128 devices in a mesh: tm: 8 (over z, core), space: 16 (over x, y).
Axes of the slice: x: 4, y: 4, z: 4, core: 2. Of those that a mesh axis runs over, the one named last changes fastest.
Arguments:
- video_tokens: bfloat16 [128, 256, 1408], P(('tm', 'space')), may hold values from -8 to 8
- grad_rows: bfloat16 [8, 16, 8, 64, 1408], P('tm', 'space'), may hold values from -6 to 6
- targets: int32 [8, 16, 8, 64], P('tm', 'space'), may hold values from 0 to 255, as said below
- counts: int32 [8, 16, 8], P('tm', 'space'), may hold values from 0 to 64, as said below
- attend_space: bfloat16 [1408, 2112], replicated, may hold values from -1 to 1
- output_space: bfloat16 [1408, 704], replicated, may hold values from -0.21875 to 0.21875
- attend_time: bfloat16 [1408, 2112], replicated, may hold values from -1 to 1
- output_time: bfloat16 [1408, 704], replicated, may hold values from -0.21875 to 0.21875
Outputs:
- token_grad: bfloat16 [128, 256, 1408], P(('tm', 'space'))
- space_grad: float32 [1408, 704], P(('tm', 'space'))
- time_grad: float32 [1408, 704], P(('tm', 'space'))
The draws below stay inside these ranges and needn't reach their ends.
Inputs may be any that keep to these rules, and one draw needn't show every extreme that they name: For every receiver (r, s) the counts counts[o, s, r] over the owners o add up to 256, and exactly one owner sends 64 rows to it. Over the slots j < counts[o, s, r] of all owners o, targets[o, s, r, j] names each of receiver (r, s)'s 256 tokens exactly once; other slots hold arbitrary indices and are ignored.
All inputs are finite; a program needn't handle non-finite values.
Results may differ from the reference program's by a relative error of at most 0.018.
The reference program's roundings to bfloat16 on the way count: a program that leaves them out, or rounds other values in their place, can miss the bound.
Values may be sent and summed in bfloat16 or wider, within the bound.
No kernel may reach another device: no remote copies, remote signals or barrier semaphores. Data moves between devices by JAX's collectives and lax.ppermute only.
A program may use at most 128 MiB of HBM per device.

```python
import math
import jax
import jax.numpy as jnp
from jax import lax

D = 1408
HEADS = 8
HEAD = 88
P_SIZE = 256
FRAMES = 32
G = 128
CLIPS = 4
TOK_DEV = 256
CAP = 64
N_TM = 8
N_SPACE = 16


def route_plan(key):
    key_heavy, key_share, key_order, key_junk = jax.random.split(key, 4)
    shape_three = (N_TM, N_SPACE, N_TM)
    heavy_owner = jax.random.randint(key_heavy, (N_TM, N_SPACE, 1), 0, N_TM)
    owner_index = lax.broadcasted_iota(jnp.int32, shape_three, 2)
    shares = jax.random.randint(key_share, shape_three, 4, 9)
    shares = jnp.where(owner_index == heavy_owner, 0, shares)
    spare_rows = TOK_DEV - CAP
    light_rows = spare_rows * shares // jnp.sum(shares, axis=2, keepdims=True)
    first_light = jnp.where(heavy_owner == 0, 1, 0)
    leftover = spare_rows - jnp.sum(light_rows, axis=2, keepdims=True)
    light_rows = light_rows + jnp.where(owner_index == first_light, leftover, 0)
    amount = jnp.where(owner_index == heavy_owner, CAP, light_rows).astype(jnp.int32)
    offset = jnp.cumsum(amount, axis=2) - amount
    slot_index = lax.broadcasted_iota(jnp.int32, shape_three + (CAP,), 3)
    token_iota = lax.broadcasted_iota(jnp.int32, (N_TM, N_SPACE, TOK_DEV), 2)
    sort_score = jax.random.randint(key_order, (N_TM, N_SPACE, TOK_DEV), 0, 1 << 20) * TOK_DEV + token_iota
    permuted = jnp.argsort(sort_score, axis=2, stable=True).astype(jnp.int32)
    pick_index = jnp.minimum(offset[..., None] + slot_index, TOK_DEV - 1).astype(jnp.int32)
    spread_perm = jnp.broadcast_to(permuted[:, :, None, :], shape_three + (TOK_DEV,))
    picked = jnp.take_along_axis(spread_perm, pick_index, axis=3)
    filler = jax.random.randint(key_junk, shape_three + (CAP,), 0, TOK_DEV)
    target_rows = jnp.where(slot_index < amount[..., None], picked, filler).astype(jnp.int32)
    return (jnp.transpose(amount, (2, 1, 0)), jnp.transpose(target_rows, (2, 1, 0, 3)))


def projection_weight(key):
    columns_all = 3 * HEADS * HEAD
    return jnp.clip(jax.random.normal(key, (D, columns_all), jnp.float32), -6.0, 6.0) * D ** (-0.5)


def draw_counts(key, part):
    planned = route_plan(key)
    return planned[0]


def draw_targets(key, part):
    planned = route_plan(key)
    return planned[1]


def draw_video_tokens(key, part):
    key = jax.random.fold_in(key, 7)
    key_noise = jax.random.fold_in(key, 0)
    return jnp.clip(jax.random.normal(key_noise, (G, P_SIZE, D), jnp.float32), -6.0, 6.0).astype(jnp.bfloat16)


def draw_attend_space(key, part):
    key = jax.random.fold_in(key, 11)
    weights_raw = projection_weight(key)
    return weights_raw.astype(jnp.bfloat16)


def draw_attend_time(key, part):
    key = jax.random.fold_in(key, 13)
    weights_raw = projection_weight(key)
    return weights_raw.astype(jnp.bfloat16)


def block_levels(stream_key, dims, shards, smallest, top_value):
    def one(axis_at, shards_of):
        draws = jax.random.uniform(jax.random.fold_in(jax.random.fold_in(stream_key, 6), axis_at), (shards_of,), jnp.float32, smallest / len(shards), top_value / len(shards))
        return jnp.repeat(jnp.exp(draws), dims[axis_at] // shards_of).reshape((-1,) + (1,) * (len(dims) - axis_at - 1))

    gain = one(*shards[0])
    for cut in shards[1:]:
        gain = gain * one(*cut)
    return gain


def centred(key, dims, spread, bound, cuts=(), kind=jnp.bfloat16):
    values = jax.random.normal(key, dims, jnp.float32) * spread
    if len(cuts) > 0:
        values = block_levels(key, dims, cuts, -0.22, 0.18) * values
    return jnp.clip(values, min=-bound, max=bound).astype(kind)


def setup_inputs(seed: int = 0) -> dict:
    key_of = jax.random.split(jax.random.key(seed), 9)
    video_tokens = draw_video_tokens(jax.random.fold_in(key_of[8], 71), 0)
    grad_rows = centred(key_of[1], (N_TM, N_SPACE, N_TM, CAP, D), 1.0, 6.0, ((0, 8), (1, 16)))
    targets = draw_targets(jax.random.fold_in(key_of[8], 71), 0)
    counts = draw_counts(jax.random.fold_in(key_of[8], 71), 0)
    attend_space = draw_attend_space(jax.random.fold_in(key_of[8], 71), 0)
    output_space = centred(key_of[5], (D, HEADS * HEAD), (HEADS * HEAD) ** -0.5, 0.21875)
    attend_time = draw_attend_time(jax.random.fold_in(key_of[8], 71), 0)
    output_time = centred(key_of[7], (D, HEADS * HEAD), (HEADS * HEAD) ** -0.5, 0.21875)
    return dict(video_tokens=video_tokens, grad_rows=grad_rows, targets=targets, counts=counts, attend_space=attend_space, output_space=output_space, attend_time=attend_time, output_time=output_time)


def sublayer(stream, attend, output):
    widened = stream.astype(jnp.float32)
    center = lax.optimization_barrier(jnp.mean(widened, axis=-1, keepdims=True))
    centered = widened - center
    variance = lax.optimization_barrier(jnp.mean(centered * centered, axis=-1, keepdims=True))
    normed = (centered * lax.rsqrt(variance + 1e-05)).astype(jnp.bfloat16)
    projected = jnp.dot(normed, attend, preferred_element_type=jnp.float32).astype(jnp.bfloat16)
    projected = projected.reshape(stream.shape[:-1] + (3, HEADS, HEAD))
    query_rows = projected[..., 0, :, :].astype(jnp.float32)
    key_rows = projected[..., 1, :, :].astype(jnp.float32)
    value_rows = projected[..., 2, :, :].astype(jnp.float32)
    scores = jnp.einsum('blmhe,bkmhe->bmhlk', query_rows, key_rows) * HEAD ** (-0.5)
    row_max = lax.optimization_barrier(jnp.max(scores, axis=-1, keepdims=True))
    weights = jnp.exp(scores - row_max)
    attn_probs = (weights / lax.optimization_barrier(jnp.sum(weights, axis=-1, keepdims=True))).astype(jnp.bfloat16)
    mixed = jnp.einsum('bmhlk,bkmhe->blmhe', attn_probs.astype(jnp.float32), value_rows)
    mixed = mixed.astype(jnp.bfloat16).reshape(stream.shape[:-1] + (HEADS * HEAD,))
    branch = lax.dot_general(mixed, output, (((mixed.ndim - 1,), (1,)), ((), ())), preferred_element_type=jnp.float32)
    return ((widened + branch).astype(jnp.bfloat16), mixed)

def reference(video_tokens, grad_rows, targets, counts, attend_space, output_space, attend_time, output_time):

    def route(dest):
        rows = jnp.swapaxes(grad_rows[:, :, dest], 0, 1).reshape(N_SPACE, N_TM * CAP, D)
        aimed = jnp.swapaxes(targets[:, :, dest], 0, 1).reshape(N_SPACE, N_TM * CAP)
        allowed = jnp.swapaxes(counts[:, :, dest], 0, 1)
        slot_index = lax.broadcasted_iota(jnp.int32, (N_SPACE, N_TM, CAP), 2)
        valid = (slot_index < allowed[:, :, None]).reshape(N_SPACE, N_TM * CAP)
        token_index = lax.broadcasted_iota(jnp.int32, (N_SPACE, TOK_DEV, N_TM * CAP), 1)
        matches = (aimed[:, None, :] == token_index) & valid[:, None, :]
        return jnp.einsum('stk,skd->std', matches.astype(jnp.float32), rows.astype(jnp.float32)).astype(jnp.bfloat16)
    grad_out = lax.map(route, jnp.arange(N_TM, dtype=jnp.int32)).reshape(G, P_SIZE, D)
    frame_block = math.gcd(G, 8)

    def space_forward(block):
        return sublayer(block[:, :, None, :], attend_space, output_space)[0][:, :, 0, :]
    hidden = lax.map(space_forward, video_tokens.reshape(G // frame_block, frame_block, P_SIZE, D)).reshape(G, P_SIZE, D)
    patch_block = math.gcd(P_SIZE, 16)

    def arrange(field):
        return jnp.moveaxis(field.reshape(CLIPS, FRAMES, P_SIZE // patch_block, patch_block, D), 2, 0)

    def time_backward(operands):
        block, cotangent = operands

        def layer(stream):
            return sublayer(stream, attend_time, output_time)
        layer_out, pullback, mixed = jax.vjp(layer, block, has_aux=True)
        grad_in = pullback(cotangent)[0]
        partial_sum = jnp.dot(cotangent.reshape(-1, D).T, mixed.reshape(-1, HEADS * HEAD), preferred_element_type=jnp.float32)
        return (grad_in, partial_sum)
    grad_blocks, time_parts = lax.map(time_backward, (arrange(hidden), arrange(grad_out)))
    grad_hidden = jnp.moveaxis(grad_blocks, 0, 2).reshape(G, P_SIZE, D)
    time_grad = lax.optimization_barrier(jnp.sum(time_parts, axis=0))

    def space_backward(operands):
        block, cotangent = operands

        def layer(stream):
            return sublayer(stream, attend_space, output_space)
        layer_out, pullback, mixed = jax.vjp(layer, block[:, :, None, :], has_aux=True)
        grad_in = pullback(cotangent[:, :, None, :])[0][:, :, 0, :]
        partial_sum = jnp.dot(cotangent.reshape(-1, D).T, mixed.reshape(-1, HEADS * HEAD), preferred_element_type=jnp.float32)
        return (grad_in, partial_sum)
    token_blocks, space_parts = lax.map(space_backward, (video_tokens.reshape(G // frame_block, frame_block, P_SIZE, D), grad_hidden.reshape(G // frame_block, frame_block, P_SIZE, D)))
    token_grad = token_blocks.reshape(G, P_SIZE, D)
    space_grad = lax.optimization_barrier(jnp.sum(space_parts, axis=0))
    return (token_grad, space_grad, time_grad)
```

```python
import jax
import jax.numpy as jnp
from jax import lax
from jax.sharding import Mesh
from jax.sharding import PartitionSpec as P

HEADS = 8
HEAD = 88


def sublayer(stream, attend, output):
    widened = stream.astype(jnp.float32)
    center = jnp.mean(widened, axis=-1, keepdims=True)
    centered = widened - center
    variance = jnp.mean(centered * centered, axis=-1, keepdims=True)
    normed = (centered * lax.rsqrt(variance + 1e-05)).astype(jnp.bfloat16)
    projected = jnp.dot(normed, attend, preferred_element_type=jnp.float32).astype(jnp.bfloat16)
    projected = projected.reshape(stream.shape[:-1] + (3, HEADS, HEAD))
    query_rows = projected[..., 0, :, :]
    key_rows = projected[..., 1, :, :]
    value_rows = projected[..., 2, :, :]
    scores = jnp.einsum(
        "blmhe,bkmhe->bmhlk", query_rows, key_rows, preferred_element_type=jnp.float32
    ) * HEAD ** (-0.5)
    row_max = jnp.max(scores, axis=-1, keepdims=True)
    weights = jnp.exp(scores - row_max)
    attn_probs = (weights / jnp.sum(weights, axis=-1, keepdims=True)).astype(jnp.bfloat16)
    mixed = jnp.einsum(
        "bmhlk,bkmhe->blmhe", attn_probs, value_rows, preferred_element_type=jnp.float32
    )
    mixed = mixed.astype(jnp.bfloat16).reshape(stream.shape[:-1] + (HEADS * HEAD,))
    branch = lax.dot_general(
        mixed, output, (((mixed.ndim - 1,), (1,)), ((), ())), preferred_element_type=jnp.float32
    )
    return ((widened + branch).astype(jnp.bfloat16), mixed)


def summed_share(partial):
    rows, columns = partial.shape
    chips, cores, space = lax.axis_size("z"), lax.axis_size("core"), lax.axis_size("space")
    share = rows // (chips * cores * space)
    sent = partial.astype(jnp.bfloat16).reshape(chips, cores, space * share, columns)
    sent = jnp.swapaxes(sent, 0, 1)
    for axis, count in (("core", cores), ("z", chips)):
        sent = sent.reshape(count, -1, columns)
        got = lax.all_to_all(sent, axis, split_axis=0, concat_axis=0, tiled=True)
        sent = jnp.sum(got.astype(jnp.float32), axis=0).astype(jnp.bfloat16)
    sent = jnp.pad(sent.reshape(space, share, columns), ((0, 0), (0, 5), (0, 0)))
    got = lax.all_to_all(sent, "space", split_axis=0, concat_axis=0, tiled=True)
    return jnp.sum(got.astype(jnp.float32), axis=0)[:share]


CLIP = ("core", "space")


def to_patches(frame):
    devices = lax.axis_size(CLIP)
    cut = frame.reshape(devices, frame.shape[1] // devices, frame.shape[2])
    return lax.all_to_all(cut, CLIP, split_axis=0, concat_axis=0, tiled=True)


def body(
    video_tokens, grad_rows, targets, counts, attend_space, output_space, attend_time, output_time
):
    owners = lax.axis_size(("z", "core"))
    frames_dev, patches, model_width = video_tokens.shape
    capacity = grad_rows.shape[3]
    routed = ("z", "core")
    rows = lax.all_to_all(
        grad_rows.reshape(owners, capacity, model_width), routed, split_axis=0, concat_axis=0, tiled=True
    )
    aimed = targets.reshape(owners, capacity)
    slot = lax.broadcasted_iota(jnp.int32, aimed.shape, 1)
    aimed = jnp.where(slot < counts.reshape(owners, 1), aimed, -1)
    aimed = lax.all_to_all(aimed, routed, split_axis=0, concat_axis=0, tiled=True)
    token = lax.broadcasted_iota(jnp.int32, (patches, owners * capacity), 0)
    matches = (aimed.reshape(1, -1) == token).astype(jnp.bfloat16)
    grad_out = jnp.dot(
        matches, rows.reshape(-1, model_width), preferred_element_type=jnp.float32
    ).astype(jnp.bfloat16)

    def space_layer(stream):
        return sublayer(stream, attend_space, output_space)

    def time_layer(stream):
        return sublayer(stream, attend_time, output_time)

    hidden_four, space_pull, space_mixed = jax.vjp(
        space_layer, video_tokens[:, :, None, :], has_aux=True
    )
    patch_hidden = to_patches(hidden_four[:, :, 0, :])
    patch_grad = to_patches(grad_out[None])
    layer_out, time_pull, time_mixed = jax.vjp(time_layer, patch_hidden[None], has_aux=True)
    grad_time_input = time_pull(patch_grad[None])[0][0]
    time_part = lax.dot_general(
        patch_grad.reshape(-1, model_width),
        time_mixed.reshape(-1, HEADS * HEAD),
        (((0,), (0,)), ((), ())),
        preferred_element_type=jnp.float32,
    )
    grad_hidden = lax.all_to_all(grad_time_input, CLIP, split_axis=0, concat_axis=0, tiled=True)
    grad_hidden = grad_hidden.reshape(1, patches, model_width)
    space_part = lax.dot_general(
        grad_hidden.reshape(-1, model_width),
        space_mixed.reshape(-1, HEADS * HEAD),
        (((0,), (0,)), ((), ())),
        preferred_element_type=jnp.float32,
    )
    time_grad = summed_share(time_part)
    space_grad = summed_share(space_part)
    token_grad = space_pull(grad_hidden[:, :, None, :])[0][:, :, 0, :]
    return (token_grad, space_grad, time_grad)


def solution(mesh):
    chips = mesh.shape["tm"] // 2
    fine = Mesh(
        mesh.devices.reshape(chips, 2, mesh.shape["space"]), ("z", "core", "space")
    )
    tm = ("z", "core")
    whole = ("z", "core", "space")
    in_specs = (
        P(whole, None, None),
        P(tm, "space", None, None, None),
        P(tm, "space", None, None),
        P(tm, "space", None),
        P(),
        P(),
        P(),
        P(),
    )
    out_specs = (P(whole, None, None), P(whole, None), P(whole, None))
    return jax.shard_map(body, mesh=fine, in_specs=in_specs, out_specs=out_specs, check_vma=False)
```

```python
import jax, jax.numpy as jnp
from jax import lax
from jax.experimental import pallas as pl
from jax.experimental.pallas import tpu as pltpu
from jax.sharding import Mesh
from jax.sharding import PartitionSpec as P

HEADS = 8
HEAD = 88
EPS = 1e-05
PATCHES = 8
CLIP = ("core", "space")
OWNERS = ("z", "core")
VMEM = pl.BlockSpec(memory_space=pltpu.VMEM)
SMEM = pl.BlockSpec(memory_space=pltpu.SMEM)


LIMIT = pltpu.CompilerParams(vmem_limit_bytes=40 * 2**20)


def cost(flops):
    return pl.CostEstimate(flops=int(flops), bytes_accessed=10_000_000, transcendentals=600_000)


def normalise(stream):
    widened = stream.astype(jnp.float32)
    center = jnp.mean(widened, axis=-1, keepdims=True)
    centered = widened - center
    variance = jnp.mean(centered * centered, axis=-1, keepdims=True)
    scale = lax.rsqrt(variance + EPS)
    return centered * scale, scale


def dot_nt(a, b):
    return lax.dot_general(a, b, (((1,), (1,)), ((), ())), preferred_element_type=jnp.float32)


def dot_tn(a, b):
    return lax.dot_general(a, b, (((0,), (0,)), ((), ())), preferred_element_type=jnp.float32)


def dot_nn(a, b):
    return jnp.dot(a, b, preferred_element_type=jnp.float32)


def same_patch(tokens):
    row = lax.broadcasted_iota(jnp.int32, (tokens, tokens), 0)
    column = lax.broadcasted_iota(jnp.int32, (tokens, tokens), 1)
    return (row % PATCHES) == (column % PATCHES)


def head(projected_ref, part, h):
    at = (part * HEADS + h) * HEAD
    return projected_ref[:, at : at + HEAD]


def forward_kernel(temporal, stream_ref, attend_ref, *rest):
    if temporal:
        projected_ref, probs_ref, mixed_ref = rest
    else:
        output_ref, projected_ref, probs_ref, mixed_ref, out_ref = rest
    tokens = stream_ref.shape[0]
    normed = normalise(stream_ref[...])[0].astype(jnp.bfloat16)
    projected_ref[...] = dot_nt(normed, attend_ref[...]).astype(jnp.bfloat16)
    for h in range(HEADS):
        scores = dot_nt(head(projected_ref, 0, h), head(projected_ref, 1, h)) * HEAD**-0.5
        if temporal:
            scores = jnp.where(same_patch(tokens), scores, -jnp.inf)
        weights = jnp.exp(scores - jnp.max(scores, axis=-1, keepdims=True))
        probs = (weights / jnp.sum(weights, axis=-1, keepdims=True)).astype(jnp.bfloat16)
        probs_ref[h] = probs
        mixed_ref[:, h * HEAD : (h + 1) * HEAD] = dot_nn(probs, head(projected_ref, 2, h)).astype(
            jnp.bfloat16
        )
    if not temporal:
        branch = dot_nn(mixed_ref[...], output_ref[...])
        out_ref[...] = (stream_ref[...].astype(jnp.float32) + branch).astype(jnp.bfloat16)


def forward(stream, attend, output=None):
    temporal = output is None
    tokens, width = stream.shape
    bf = jnp.bfloat16
    shapes = [
        jax.ShapeDtypeStruct((tokens, 3 * HEADS * HEAD), bf),
        jax.ShapeDtypeStruct((HEADS, tokens, tokens), bf),
        jax.ShapeDtypeStruct((tokens, HEADS * HEAD), bf),
    ]
    args = [stream, attend.T]
    if not temporal:
        shapes.append(jax.ShapeDtypeStruct((tokens, width), bf))
        args.append(output.T)
    return pl.pallas_call(
        lambda *refs: forward_kernel(temporal, *refs),
        out_shape=shapes,
        in_specs=[VMEM] * len(args),
        out_specs=[VMEM] * len(shapes),
        compiler_params=LIMIT,
        cost_estimate=cost(2.2e9),
        name="time_forward" if temporal else "space_forward",
    )(*args)


def backward_kernel(grad_ref, stream_ref, projected_ref, probs_ref, attend_ref, output_ref, out_ref, dproj_ref):
    bf = jnp.bfloat16
    grad = grad_ref[...]
    dmixed = dot_nt(grad, output_ref[...]).astype(bf)
    for h in range(HEADS):
        probs = probs_ref[h]
        dm = dmixed[:, h * HEAD : (h + 1) * HEAD]
        dprobs = dot_nt(dm, head(projected_ref, 2, h)).astype(bf).astype(jnp.float32)
        wide = probs.astype(jnp.float32)
        scaled = wide * dprobs
        dscores = (scaled - wide * jnp.sum(scaled, axis=-1, keepdims=True)) * HEAD**-0.5
        dscores = dscores.astype(bf)
        for part, value in (
            (0, dot_nn(dscores, head(projected_ref, 1, h))),
            (1, dot_tn(dscores, head(projected_ref, 0, h))),
            (2, dot_tn(probs, dm)),
        ):
            at = (part * HEADS + h) * HEAD
            dproj_ref[:, at : at + HEAD] = value.astype(bf)
    dnormed = dot_nn(dproj_ref[...], attend_ref[...]).astype(bf).astype(jnp.float32)
    normed, scale = normalise(stream_ref[...])
    mean_d = jnp.mean(dnormed, axis=-1, keepdims=True)
    mean_dn = jnp.mean(dnormed * normed, axis=-1, keepdims=True)
    inner = scale * (dnormed - mean_d - normed * mean_dn)
    out_ref[...] = (grad.astype(jnp.float32) + inner).astype(bf)


def backward(grad, stream, projected, probs, attend, output, name):
    args = [grad, stream, projected, probs, attend.T, output.T]
    return pl.pallas_call(
        backward_kernel,
        out_shape=jax.ShapeDtypeStruct(grad.shape, jnp.bfloat16),
        in_specs=[VMEM] * len(args),
        out_specs=VMEM,
        scratch_shapes=[pltpu.VMEM(projected.shape, jnp.bfloat16)],
        compiler_params=LIMIT,
        cost_estimate=cost(2.6e9),
        name=name,
    )(*args)


def weight_kernel(grad_ref, mixed_ref, out_ref):
    out_ref[...] = dot_tn(grad_ref[...], mixed_ref[...]).astype(jnp.bfloat16)


def weight_partial(grad, mixed, name):
    return pl.pallas_call(
        weight_kernel,
        out_shape=jax.ShapeDtypeStruct((grad.shape[1], mixed.shape[1]), jnp.bfloat16),
        in_specs=[VMEM] * 2,
        out_specs=VMEM,
        compiler_params=LIMIT,
        name=name,
    )(grad, mixed)


def weight_split_kernel(place_ref, grad_ref, mixed_ref, mine_ref, other_ref, total_ref):
    core = place_ref[1]
    chips, rows, _ = mine_ref.shape
    total_ref[...] = dot_tn(grad_ref[...], mixed_ref[...])
    for z in range(chips):
        for ref, of in ((mine_ref, core), (other_ref, 1 - core)):
            at = pl.multiple_of((2 * z + of) * rows, 8)
            ref[z] = total_ref[pl.ds(at, rows), :].astype(jnp.bfloat16)


def weight_split(place, grad, mixed, chips, name):
    rows, columns = grad.shape[1], mixed.shape[1]
    half = jax.ShapeDtypeStruct((chips, rows // (2 * chips), columns), jnp.bfloat16)
    return pl.pallas_call(
        weight_split_kernel,
        out_shape=[half, half],
        in_specs=[SMEM, VMEM, VMEM],
        out_specs=[VMEM] * 2,
        scratch_shapes=[pltpu.VMEM((rows, columns), jnp.float32)],
        compiler_params=LIMIT,
        name=name,
    )(place, grad, mixed)


def pack_kernel(space_ref, time_ref, out_ref):
    devices = out_ref.shape[0]
    total = space_ref[0].astype(jnp.float32)
    for z in range(1, space_ref.shape[0]):
        total = total + space_ref[z].astype(jnp.float32)
    both = jnp.concatenate([total, time_ref[...].astype(jnp.float32)], axis=1)
    share = both.shape[0] // devices
    fill = jnp.zeros((out_ref.shape[1] - share, both.shape[1]), jnp.float32)
    for s in range(devices):
        rows = jnp.concatenate([both[s * share : (s + 1) * share, :], fill], axis=0)
        out_ref[s] = rows.astype(jnp.bfloat16)


def pack(space_parts, time_part, devices):
    columns = time_part.shape[1]
    return pl.pallas_call(
        pack_kernel,
        out_shape=jax.ShapeDtypeStruct((devices, 16, 2 * columns), jnp.bfloat16),
        in_specs=[VMEM] * 2,
        out_specs=VMEM,
        compiler_params=LIMIT,
        name="pack_shares",
    )(space_parts, time_part)


def unpack_kernel(parts_ref, space_ref, time_ref):
    share, columns = space_ref.shape
    total = parts_ref[0].astype(jnp.float32)
    for s in range(1, parts_ref.shape[0]):
        total = total + parts_ref[s].astype(jnp.float32)
    space_ref[...] = total[:share, :columns]
    time_ref[...] = total[:share, columns:]


def unpack(parts, share):
    out = jax.ShapeDtypeStruct((share, parts.shape[2] // 2), jnp.float32)
    return pl.pallas_call(
        unpack_kernel,
        out_shape=[out, out],
        in_specs=[VMEM],
        out_specs=[VMEM] * 2,
        compiler_params=LIMIT,
        name="sum_shares",
    )(parts)


def scatter_kernel(place_ref, aimed_ref, *refs):
    out_ref = refs[-1]
    z, core = place_ref[0], place_ref[1]
    chips = len(refs) - 1
    tokens = out_ref.shape[0]
    total = None
    for d in range(chips):
        source = (z + chips - d) % chips
        aims = [aimed_ref[(source * 2 + of) * 2 * chips + z * 2 + core] for of in (core, 1 - core)]
        aims = jnp.concatenate(aims, axis=1)
        token = lax.broadcasted_iota(jnp.int32, (tokens, aims.shape[1]), 0)
        matches = jnp.where(aims == token, 1.0, 0.0).astype(jnp.bfloat16)
        term = dot_nn(matches, refs[d][...])
        total = term if total is None else total + term
    out_ref[...] = total.astype(jnp.bfloat16)


def scatter_rows(place, aimed, pieces, tokens):
    return pl.pallas_call(
        scatter_kernel,
        out_shape=jax.ShapeDtypeStruct((tokens, pieces[0].shape[1]), jnp.bfloat16),
        in_specs=[SMEM] + [VMEM] * (1 + len(pieces)),
        out_specs=VMEM,
        compiler_params=LIMIT,
        cost_estimate=cost(4e8),
        name="scatter_rows",
    )(place, aimed, *pieces)


def exchange(tokens, axes):
    devices = lax.axis_size(axes)
    cut = tokens.reshape(devices, tokens.shape[0] // devices, tokens.shape[1])
    return lax.all_to_all(cut, axes, split_axis=0, concat_axis=0, tiled=True).reshape(tokens.shape)


def shift(array, axis, by):
    devices = lax.axis_size(axis)
    return lax.ppermute(array, axis, [(i, (i + by) % devices) for i in range(devices)])


def routed(grad_rows, targets, counts, place, tokens):
    chips, cores = lax.axis_size("z"), lax.axis_size("core")
    capacity, width = grad_rows.shape[3:]
    z, core = place[0], place[1]
    rows = grad_rows.reshape(chips, cores, capacity, width)
    aimed = targets.reshape(chips * cores, 1, capacity)
    slot = lax.broadcasted_iota(jnp.int32, aimed.shape, 2)
    aimed = jnp.where(slot < counts.reshape(-1, 1, 1), aimed, -1)
    aimed = lax.all_gather(aimed, OWNERS, axis=0, tiled=True)

    def of_core(which):
        return lax.dynamic_index_in_dim(rows, which, axis=1, keepdims=False)

    got = shift(of_core(1 - core), "core", 1)
    mine = of_core(core)
    pieces = []
    for d in range(chips):
        to = (z + d) % chips
        block = [lax.dynamic_index_in_dim(a, to, axis=0, keepdims=False) for a in (mine, got)]
        block = jnp.concatenate(block, axis=0)
        pieces.append(block if d == 0 else shift(block, "z", d))
    return scatter_rows(place, aimed, pieces, tokens)


def body(
    video_tokens, grad_rows, targets, counts, attend_space, output_space, attend_time, output_time
):
    chips, space = lax.axis_size("z"), lax.axis_size("space")
    stream = video_tokens[0]
    place = jnp.stack([lax.axis_index("z"), lax.axis_index("core")]).astype(jnp.int32)
    grad_out = routed(grad_rows, targets, counts, place, stream.shape[0])
    space_saved = forward(stream, attend_space, output_space)
    hidden = exchange(space_saved[3], CLIP)
    grad = exchange(grad_out, CLIP)
    time_saved = forward(hidden, attend_time)
    grad_hidden = backward(
        grad, hidden, time_saved[0], time_saved[1], attend_time, output_time, "time_backward"
    )
    time_part = weight_partial(grad, time_saved[2], "time_weight")
    time_part = lax.psum_scatter(time_part, OWNERS, scatter_dimension=0, tiled=True)
    grad_hidden = exchange(grad_hidden, CLIP)
    mine, other = weight_split(place, grad_hidden, space_saved[2], chips, "space_weight")
    space_part = mine.astype(jnp.float32) + shift(other, "core", 1).astype(jnp.float32)
    space_part = space_part.astype(jnp.bfloat16)
    space_part = lax.all_to_all(space_part, "z", split_axis=0, concat_axis=0, tiled=True)
    shares = pack(space_part, time_part, space)
    shares = lax.all_to_all(shares, "space", split_axis=0, concat_axis=0, tiled=True)
    space_grad, time_grad = unpack(shares, time_part.shape[0] // space)
    token_grad = backward(
        grad_hidden, stream, space_saved[0], space_saved[1], attend_space, output_space, "space_backward"
    )
    return (token_grad[None], space_grad, time_grad)


def solution(mesh):
    chips = mesh.shape["tm"] // 2
    fine = Mesh(mesh.devices.reshape(chips, 2, mesh.shape["space"]), ("z", "core", "space"))
    whole = ("z", "core", "space")
    in_specs = (
        P(whole, None, None),
        P(OWNERS, "space", None, None, None),
        P(OWNERS, "space", None, None),
        P(OWNERS, "space", None),
        P(),
        P(),
        P(),
        P(),
    )
    out_specs = (P(whole, None, None), P(whole, None), P(whole, None))
    return jax.shard_map(body, mesh=fine, in_specs=in_specs, out_specs=out_specs, check_vma=False)
```

```python
import jax, jax.numpy as jnp
from jax import lax
from jax.experimental import pallas as pl
from jax.experimental.pallas import tpu as pltpu
from jax.sharding import Mesh
from jax.sharding import PartitionSpec as P

HEADS = 8
HEAD = 88
EPS = 1e-05
PATCHES = 8
WIDE = HEADS * HEAD
CLIP = ("core", "space")
OWNERS = ("z", "core")
VMEM = pl.BlockSpec(memory_space=pltpu.VMEM)
SMEM = pl.BlockSpec(memory_space=pltpu.SMEM)


LIMIT = pltpu.CompilerParams(vmem_limit_bytes=16 * 2**20)


def cost(flops):
    return pl.CostEstimate(flops=int(flops), bytes_accessed=10_000_000, transcendentals=600_000)


def normalise(stream):
    widened = stream.astype(jnp.float32)
    center = jnp.mean(widened, axis=-1, keepdims=True)
    centered = widened - center
    variance = jnp.mean(centered * centered, axis=-1, keepdims=True)
    scale = lax.rsqrt(variance + EPS)
    return centered * scale, scale


def dot_nt(a, b):
    return lax.dot_general(a, b, (((1,), (1,)), ((), ())), preferred_element_type=jnp.float32)


def dot_tn(a, b):
    return lax.dot_general(a, b, (((0,), (0,)), ((), ())), preferred_element_type=jnp.float32)


def dot_nn(a, b):
    return jnp.dot(a, b, preferred_element_type=jnp.float32)


def same_patch(tokens):
    row = lax.broadcasted_iota(jnp.int32, (tokens, tokens), 0)
    column = lax.broadcasted_iota(jnp.int32, (tokens, tokens), 1)
    return (row % PATCHES) == (column % PATCHES)


def head(projected_ref, part, h):
    at = (part * HEADS + h) * HEAD
    return projected_ref[:, at : at + HEAD]


def forward_kernel(temporal, stream_ref, attend_ref, *rest):
    if temporal:
        projected_ref, probs_ref, mixed_ref = rest
    else:
        output_ref, projected_ref, probs_ref, mixed_ref, out_ref = rest
    tokens = stream_ref.shape[0]
    normed = normalise(stream_ref[...])[0].astype(jnp.bfloat16)
    projected_ref[...] = dot_nt(normed, attend_ref[...]).astype(jnp.bfloat16)
    for h in range(HEADS):
        scores = dot_nt(head(projected_ref, 0, h), head(projected_ref, 1, h)) * HEAD**-0.5
        if temporal:
            scores = jnp.where(same_patch(tokens), scores, -jnp.inf)
        weights = jnp.exp(scores - jnp.max(scores, axis=-1, keepdims=True))
        probs = (weights / jnp.sum(weights, axis=-1, keepdims=True)).astype(jnp.bfloat16)
        probs_ref[h] = probs
        mixed_ref[:, h * HEAD : (h + 1) * HEAD] = dot_nn(probs, head(projected_ref, 2, h)).astype(
            jnp.bfloat16
        )
    if not temporal:
        branch = dot_nn(mixed_ref[...], output_ref[...])
        out_ref[...] = (stream_ref[...].astype(jnp.float32) + branch).astype(jnp.bfloat16)


def forward(stream, attend, output=None):
    temporal = output is None
    tokens, width = stream.shape
    bf = jnp.bfloat16
    shapes = [
        jax.ShapeDtypeStruct((tokens, 3 * HEADS * HEAD), bf),
        jax.ShapeDtypeStruct((HEADS, tokens, tokens), bf),
        jax.ShapeDtypeStruct((tokens, HEADS * HEAD), bf),
    ]
    args = [stream, attend.T]
    if not temporal:
        shapes.append(jax.ShapeDtypeStruct((tokens, width), bf))
        args.append(output.T)
    return pl.pallas_call(
        lambda *refs: forward_kernel(temporal, *refs),
        out_shape=shapes,
        in_specs=[VMEM] * len(args),
        out_specs=[VMEM] * len(shapes),
        compiler_params=LIMIT,
        cost_estimate=cost(2.2e9),
        name="time_forward" if temporal else "space_forward",
    )(*args)


def backward_kernel(grad_ref, stream_ref, projected_ref, probs_ref, attend_ref, output_ref, out_ref, dproj_ref):
    bf = jnp.bfloat16
    grad = grad_ref[...]
    dmixed = dot_nt(grad, output_ref[...]).astype(bf)
    for h in range(HEADS):
        probs = probs_ref[h]
        dm = dmixed[:, h * HEAD : (h + 1) * HEAD]
        dprobs = dot_nt(dm, head(projected_ref, 2, h)).astype(bf).astype(jnp.float32)
        wide = probs.astype(jnp.float32)
        scaled = wide * dprobs
        dscores = (scaled - wide * jnp.sum(scaled, axis=-1, keepdims=True)) * HEAD**-0.5
        dscores = dscores.astype(bf)
        for part, value in (
            (0, dot_nn(dscores, head(projected_ref, 1, h))),
            (1, dot_tn(dscores, head(projected_ref, 0, h))),
            (2, dot_tn(probs, dm)),
        ):
            at = (part * HEADS + h) * HEAD
            dproj_ref[:, at : at + HEAD] = value.astype(bf)
    dnormed = dot_nn(dproj_ref[...], attend_ref[...]).astype(bf).astype(jnp.float32)
    normed, scale = normalise(stream_ref[...])
    mean_d = jnp.mean(dnormed, axis=-1, keepdims=True)
    mean_dn = jnp.mean(dnormed * normed, axis=-1, keepdims=True)
    inner = scale * (dnormed - mean_d - normed * mean_dn)
    out_ref[...] = (grad.astype(jnp.float32) + inner).astype(bf)


def backward(grad, stream, projected, probs, attend, output, name):
    args = [grad, stream, projected, probs, attend.T, output.T]
    return pl.pallas_call(
        backward_kernel,
        out_shape=jax.ShapeDtypeStruct(grad.shape, jnp.bfloat16),
        in_specs=[VMEM] * len(args),
        out_specs=VMEM,
        scratch_shapes=[pltpu.VMEM(projected.shape, jnp.bfloat16)],
        compiler_params=LIMIT,
        cost_estimate=cost(2.6e9),
        name=name,
    )(*args)


def call(kernel, outs, args, name, smem=0, flops=1e9, scratch=()):
    return pl.pallas_call(
        kernel,
        out_shape=outs,
        in_specs=[SMEM] * smem + [VMEM] * (len(args) - smem),
        out_specs=[VMEM] * len(outs) if isinstance(outs, list) else VMEM,
        scratch_shapes=scratch,
        compiler_params=LIMIT,
        cost_estimate=cost(flops),
        name=name,
    )(*args)


def bf16(*shape):
    return jax.ShapeDtypeStruct(shape, jnp.bfloat16)


def aim_kernel(place_ref, counts_ref, targets_ref, rows_ref, *piece_refs):
    chips = len(piece_refs)
    for d, piece_ref in enumerate(piece_refs):
        to = (place_ref[0] + d) % chips
        piece_ref[:128, :] = rows_ref[to]
        piece_ref[128:, :] = jnp.zeros((16, piece_ref.shape[1]), jnp.bfloat16)
        line = lax.broadcasted_iota(jnp.int32, (16, 64), 0)
        slot = lax.broadcasted_iota(jnp.int32, (16, 64), 1)
        aims = jnp.zeros((16, 64), jnp.int32)
        for core in range(2):
            valid = (line == core) & (slot < counts_ref[2 * to + core])
            row = jnp.where(valid, targets_ref[2 * to + core], -1)
            aims = jnp.where(line == core, row, aims)
        piece_ref[128:, :64] = aims.astype(jnp.float32).astype(jnp.bfloat16)


def scatter_kernel(place_ref, *refs):
    pieces, (mine_ref, other_ref) = refs[:-2], refs[-2:]
    tokens = mine_ref.shape[0]
    line = lax.broadcasted_iota(jnp.int32, (16, 64), 0)
    token = lax.broadcasted_iota(jnp.int32, (tokens, 64), 0).astype(jnp.float32)
    for out_ref, core in ((mine_ref, place_ref[1]), (other_ref, 1 - place_ref[1])):
        total = jnp.zeros(out_ref.shape, jnp.float32)
        for piece_ref in pieces:
            info = piece_ref[128:, :64].astype(jnp.float32)
            aims = jnp.sum(jnp.where(line == core, info, 0.0), axis=0, keepdims=True)
            matches = jnp.where(aims == token, 1.0, 0.0).astype(jnp.bfloat16)
            at = pl.multiple_of(core * 64, 64)
            total = total + dot_nn(matches, piece_ref[pl.ds(at, 64), :])
        out_ref[...] = total.astype(jnp.bfloat16)


def split_kernel(chips, place_ref, grad_ref, mine_ref, other_ref):
    grad = grad_ref[...]
    step = grad.shape[1] // (2 * chips)
    halves = [
        jnp.concatenate([grad[:, (2 * z + c) * step : (2 * z + c + 1) * step] for z in range(chips)], axis=1)
        for c in range(2)
    ]
    first = place_ref[1] == 0
    mine_ref[...] = jnp.where(first, halves[0], halves[1])
    other_ref[...] = jnp.where(first, halves[1], halves[0])


def split(place, grad, chips, name):
    half = bf16(grad.shape[0], grad.shape[1] // 2)
    return call(lambda *refs: split_kernel(chips, *refs), [half, half], [place, grad], name, smem=1)


def chip_product_kernel(grad_ref, mixed_ref, got_ref, out_ref):
    tokens = grad_ref.shape[0]
    total = dot_tn(grad_ref[...], mixed_ref[...]) + dot_tn(got_ref[:tokens, :], got_ref[tokens:, :])
    out_ref[...] = total.astype(jnp.bfloat16)


SHARE = 11
CUT = 640


def pack_kernel(time_ref, grad_ref, grad_got_ref, mixed_ref, mixed_got_ref, out_ref):
    space = dot_tn(grad_ref[...], mixed_ref[...]) + dot_tn(grad_got_ref[...], mixed_got_ref[...])
    time = time_ref[...].astype(jnp.float32)
    main = jnp.concatenate([time[:, :CUT], space[:, :384]], axis=1)
    left = jnp.concatenate([space[:, 384:CUT], time[:, CUT:], space[:, CUT:]], axis=1)
    zero = jnp.zeros((2, 128), jnp.float32)
    for k in range(out_ref.shape[0]):
        x = left[k * SHARE : (k + 1) * SHARE, :]
        cut = [x[:, 128 * t : 128 * (t + 1)] for t in range(3)]
        low = [part[5 * u : 5 * u + 5] for part in cut for u in range(2)]
        low.append(jnp.concatenate([part[10:] for part in cut] + [zero], axis=0))
        low.append(jnp.zeros((5, 128), jnp.float32))
        rows = [main[k * SHARE : (k + 1) * SHARE, :], jnp.concatenate(low, axis=1)]
        out_ref[k] = jnp.concatenate(rows, axis=0).astype(jnp.bfloat16)


def unpack_kernel(parts_ref, space_ref, time_ref):
    total = parts_ref[0].astype(jnp.float32)
    for k in range(1, parts_ref.shape[0]):
        total = total + parts_ref[k].astype(jnp.float32)
    low = [total[SHARE:, 128 * t : 128 * (t + 1)] for t in range(7)]
    left = [
        jnp.concatenate([low[2 * t], low[2 * t + 1], low[6][t : t + 1]], axis=0) for t in range(3)
    ]
    time_ref[...] = jnp.concatenate([total[:SHARE, :CUT], left[2][:, :64]], axis=1)
    space_ref[...] = jnp.concatenate([total[:SHARE, CUT:], left[0], left[1], left[2][:, 64:]], axis=1)


def exchange(tokens, axes):
    devices = lax.axis_size(axes)
    cut = tokens.reshape(devices, tokens.shape[0] // devices, tokens.shape[1])
    return lax.all_to_all(cut, axes, split_axis=0, concat_axis=0, tiled=True).reshape(tokens.shape)


def shift(array, axis, by):
    devices = lax.axis_size(axis)
    return lax.ppermute(array, axis, [(i, (i + by) % devices) for i in range(devices)])


def routed(grad_rows, targets, counts, place, tokens):
    chips = lax.axis_size("z")
    width = grad_rows.shape[4]
    args = [place, counts.reshape(-1), targets.reshape(2 * chips, 1, 64), grad_rows.reshape(chips, 128, width)]
    pieces = call(aim_kernel, [bf16(144, width)] * chips, args, "aim_rows", smem=2)
    pieces = [piece if d == 0 else shift(piece, "z", d) for d, piece in enumerate(pieces)]
    mine, other = call(scatter_kernel, [bf16(tokens, width)] * 2, [place, *pieces], "scatter_rows", smem=1)
    return mine + shift(other, "core", 1)


def body(
    video_tokens, grad_rows, targets, counts, attend_space, output_space, attend_time, output_time
):
    chips = lax.axis_size("z")
    stream = video_tokens[0]
    width = stream.shape[1]
    place = jnp.stack([lax.axis_index("z"), lax.axis_index("core")]).astype(jnp.int32)
    grad_out = routed(grad_rows, targets, counts, place, stream.shape[0])
    space_saved = forward(stream, attend_space, output_space)
    hidden = exchange(space_saved[3], CLIP)
    grad = exchange(grad_out, CLIP)
    time_saved = forward(hidden, attend_time)
    space_mixed_got = shift(space_saved[2], "core", 1)
    time_mine, time_other = split(place, grad, chips, "time_split")
    time_got = shift(jnp.concatenate([time_other, time_saved[2]], axis=0), "core", 1)
    grad_hidden = backward(
        grad, hidden, time_saved[0], time_saved[1], attend_time, output_time, "time_backward"
    )
    time_sum = call(
        chip_product_kernel, bf16(width // 2, WIDE), [time_mine, time_saved[2], time_got], "time_weight"
    )
    grad_hidden = exchange(grad_hidden, CLIP)
    space_mine, space_other = split(place, grad_hidden, chips, "space_split")
    space_got = shift(space_other, "core", 1)
    keepers = lax.axis_size(("z", "space"))
    packed = call(
        pack_kernel,
        bf16(keepers, 16, 1024),
        [time_sum, space_mine, space_got, space_saved[2], space_mixed_got],
        "pack_shares",
    )
    packed = lax.all_to_all(packed, ("z", "space"), split_axis=0, concat_axis=0, tiled=True)
    share = jax.ShapeDtypeStruct((SHARE, WIDE), jnp.float32)
    space_grad, time_grad = call(unpack_kernel, [share, share], [packed], "sum_shares")
    token_grad = backward(
        grad_hidden, stream, space_saved[0], space_saved[1], attend_space, output_space, "space_backward"
    )
    return (token_grad[None], space_grad, time_grad)


def solution(mesh):
    chips = mesh.shape["tm"] // 2
    fine = Mesh(mesh.devices.reshape(chips, 2, mesh.shape["space"]), ("z", "core", "space"))
    whole = ("z", "core", "space")
    in_specs = (
        P(whole, None, None),
        P(OWNERS, "space", None, None, None),
        P(OWNERS, "space", None, None),
        P(OWNERS, "space", None),
        P(),
        P(),
        P(),
        P(),
    )
    out_specs = (P(whole, None, None), P(whole, None), P(whole, None))
    return jax.shard_map(body, mesh=fine, in_specs=in_specs, out_specs=out_specs, check_vma=False)
```

```python
import jax
import jax.numpy as jnp
from jax import lax
from jax.experimental import pallas as pl
from jax.experimental.pallas import tpu as pltpu
from jax.sharding import Mesh
from jax.sharding import PartitionSpec as P

HEADS = 8
HEAD = 88
WIDE = HEADS * HEAD
EPS = 1e-05
PATCHES = 8
SHARE = 11
CUT = 640
CLIP = ("core", "space")
OWNERS = ("z", "core")
ATTEND_CUTS = ((0, 768), (768, 1344))
VMEM = pl.BlockSpec(memory_space=pltpu.VMEM)
SMEM = pl.BlockSpec(memory_space=pltpu.SMEM)
ANY = pl.BlockSpec(memory_space=pl.ANY)


def bf16(*shape):
    return jax.ShapeDtypeStruct(shape, jnp.bfloat16)


def held(*shape):
    return pltpu.VMEM(shape, jnp.bfloat16)


def call(kernel, outs, args, name, spaces, scratch=(), flops=1e6, room=20):
    spec = {"s": SMEM, "v": VMEM, "a": ANY}
    spaces = [spec[c] for c in spaces]
    many = isinstance(outs, list)
    return pl.pallas_call(
        kernel,
        out_shape=outs,
        in_specs=spaces[: len(args)],
        out_specs=spaces[len(args) :] if many else spaces[-1],
        scratch_shapes=scratch,
        compiler_params=pltpu.CompilerParams(vmem_limit_bytes=room * 2**20),
        cost_estimate=pl.CostEstimate(
            flops=int(flops), bytes_accessed=int(flops / 200), transcendentals=0
        ),
        name=name,
    )(*args)


def normalise(stream):
    widened = stream.astype(jnp.float32)
    center = jnp.mean(widened, axis=-1, keepdims=True)
    centered = widened - center
    variance = jnp.mean(centered * centered, axis=-1, keepdims=True)
    scale = lax.rsqrt(variance + EPS)
    return centered * scale, scale


def dot_nt(a, b):
    return lax.dot_general(a, b, (((1,), (1,)), ((), ())), preferred_element_type=jnp.float32)


def dot_tn(a, b):
    return lax.dot_general(a, b, (((0,), (0,)), ((), ())), preferred_element_type=jnp.float32)


def dot_nn(a, b):
    return jnp.dot(a, b, preferred_element_type=jnp.float32)


def same_patch(tokens):
    row = lax.broadcasted_iota(jnp.int32, (tokens, tokens), 0)
    column = lax.broadcasted_iota(jnp.int32, (tokens, tokens), 1)
    return (row % PATCHES) == (column % PATCHES)


def head(projected_ref, part, h):
    at = (part * HEADS + h) * HEAD
    return projected_ref[:, at : at + HEAD]


def forward_kernel(temporal, *refs):
    if temporal:
        stream_in, attend_in, projected_out, probs_out, mixed_out = refs[:5]
        stream, attend, projected, probs, mixed, sems = refs[5:]
    else:
        stream_in, attend_in, output_in, projected_out, probs_out, mixed_out, result_out = refs[:7]
        stream, attend, projected, probs, mixed, output, result, sems = refs[7:]

    def copy(source, target, at):
        return pltpu.make_async_copy(source, target, sems.at[at])

    load = copy(stream_in, stream, 0)
    load.start()
    parts = [
        copy(attend_in.at[pl.ds(a, n)], attend.at[pl.ds(a, n)], 1 + i)
        for i, (a, n) in enumerate(ATTEND_CUTS)
    ]
    for part in parts:
        part.start()
    if not temporal:
        load_output = copy(output_in, output, 4)
        load_output.start()
    load.wait()
    normed = normalise(stream[...])[0].astype(jnp.bfloat16)
    for part, (a, n) in zip(parts, ATTEND_CUTS):
        part.wait()
        projected[:, a : a + n] = dot_nt(normed, attend[a : a + n, :]).astype(jnp.bfloat16)
    stores = [copy(projected, projected_out, 5)]
    stores[0].start()
    tokens = stream.shape[0]
    if temporal:
        allowed = same_patch(tokens)
    for h in range(HEADS):
        scores = dot_nt(head(projected, 0, h), head(projected, 1, h)) * HEAD**-0.5
        if temporal:
            scores = jnp.where(allowed, scores, -jnp.inf)
        weights = jnp.exp(scores - jnp.max(scores, axis=-1, keepdims=True))
        chances = (weights / jnp.sum(weights, axis=-1, keepdims=True)).astype(jnp.bfloat16)
        probs[h] = chances
        mixed[:, h * HEAD : (h + 1) * HEAD] = dot_nn(chances, head(projected, 2, h)).astype(
            jnp.bfloat16
        )
    stores += [copy(mixed, mixed_out, 6), copy(probs, probs_out, 8)]
    stores[1].start()
    stores[2].start()
    if not temporal:
        load_output.wait()
        branch = dot_nn(mixed[...], output[...])
        result[...] = (stream[...].astype(jnp.float32) + branch).astype(jnp.bfloat16)
        stores.append(copy(result, result_out, 7))
        stores[-1].start()
    for store in stores:
        store.wait()


def forward(stream, attend, output=None):
    temporal = output is None
    tokens, width = stream.shape
    shapes = [(tokens, 3 * WIDE), (HEADS, tokens, tokens), (tokens, WIDE)]
    outs = [bf16(*shape) for shape in shapes]
    scratch = [held(tokens, width), held(3 * WIDE, width)] + [held(*shape) for shape in shapes]
    args = [stream, attend.T]
    if not temporal:
        args.append(output.T)
        outs.append(bf16(tokens, width))
        scratch += [held(WIDE, width), held(tokens, width)]
    scratch.append(pltpu.SemaphoreType.DMA((16,)))
    name = "time_forward" if temporal else "space_forward"
    spaces = "a" * (len(args) + len(outs))
    return call(lambda *refs: forward_kernel(temporal, *refs), outs, args, name, spaces, scratch, 2.2e9, 60)


def backward_kernel(
    grad_in, stream_in, projected_in, probs_in, attend_in, output_in, result_out,
    grad, stream, projected, probs, attend, output, result, dproj, sems,
):
    bf = jnp.bfloat16

    def copy(source, target, at):
        return pltpu.make_async_copy(source, target, sems.at[at])

    load_grad, load_output = copy(grad_in, grad, 0), copy(output_in, output, 1)
    load_projected = copy(projected_in, projected, 2)
    load_probs = copy(probs_in, probs, 7)
    load_attend, load_stream = copy(attend_in, attend, 3), copy(stream_in, stream, 4)
    for load in (load_grad, load_output, load_projected, load_probs, load_attend, load_stream):
        load.start()
    load_grad.wait()
    load_output.wait()
    dmixed = dot_nt(grad[...], output[...]).astype(bf)
    load_projected.wait()
    load_probs.wait()
    for h in range(HEADS):
        chances = probs[h]
        dm = dmixed[:, h * HEAD : (h + 1) * HEAD]
        dprobs = dot_nt(dm, head(projected, 2, h)).astype(bf).astype(jnp.float32)
        wide = chances.astype(jnp.float32)
        scaled = wide * dprobs
        dscores = (scaled - wide * jnp.sum(scaled, axis=-1, keepdims=True)) * HEAD**-0.5
        dscores = dscores.astype(bf)
        for part, value in (
            (0, dot_nn(dscores, head(projected, 1, h))),
            (1, dot_tn(dscores, head(projected, 0, h))),
            (2, dot_tn(chances, dm)),
        ):
            at = (part * HEADS + h) * HEAD
            dproj[:, at : at + HEAD] = value.astype(bf)
    load_attend.wait()
    load_stream.wait()
    tokens = grad.shape[0]
    for i in range(2):
        rows = slice(i * tokens // 2, (i + 1) * tokens // 2)
        dnormed = dot_nn(dproj[rows, :], attend[...]).astype(bf).astype(jnp.float32)
        normed, scale = normalise(stream[rows, :])
        mean_d = jnp.mean(dnormed, axis=-1, keepdims=True)
        mean_dn = jnp.mean(dnormed * normed, axis=-1, keepdims=True)
        inner = scale * (dnormed - mean_d - normed * mean_dn)
        result[rows, :] = (grad[rows, :].astype(jnp.float32) + inner).astype(bf)
    store = copy(result, result_out, 5)
    store.start()
    store.wait()


def backward(grad, stream, projected, probs, attend, output, name):
    args = [grad, stream, projected, probs, attend.T, output.T]
    scratch = [held(*arg.shape) for arg in args] + [held(*grad.shape), held(*projected.shape)]
    scratch.append(pltpu.SemaphoreType.DMA((16,)))
    return call(backward_kernel, bf16(*grad.shape), args, name, "a" * 7, scratch, 2.6e9, 60)


def aim_kernel(place_ref, counts_ref, targets_in, rows_in, *refs):
    piece_refs, (targets, sems) = refs[:-2], refs[-2:]
    chips = len(piece_refs)
    aimed = pltpu.make_async_copy(targets_in, targets, sems.at[chips])
    aimed.start()
    loads = []
    for d in range(chips):
        to = (place_ref[0] + d) % chips
        into = piece_refs[d].at[pl.ds(0, 128)]
        loads.append(pltpu.make_async_copy(rows_in.at[to], into, sems.at[d]))
        loads[-1].start()
    aimed.wait()
    line = lax.broadcasted_iota(jnp.int32, (16, 64), 0)
    slot = lax.broadcasted_iota(jnp.int32, (16, 64), 1)
    for d, piece_ref in enumerate(piece_refs):
        to = (place_ref[0] + d) % chips
        piece_ref[128:, :] = jnp.zeros((16, piece_ref.shape[1]), jnp.bfloat16)
        aims = jnp.full((16, 64), -1, jnp.int32)
        for core in range(2):
            valid = (line == core) & (slot < counts_ref[0, 0, 2 * to + core])
            aims = jnp.where(valid, targets[0, 0, pl.ds(2 * to + core, 1), :], aims)
        piece_ref[128:, :64] = aims.astype(jnp.float32).astype(jnp.bfloat16)
    for load in loads:
        load.wait()


def scatter_kernel(chips, place_ref, *refs):
    pieces, mine_ref, other_refs = refs[:chips], refs[chips], refs[chips + 1 :]
    tokens = mine_ref.shape[0]
    line = lax.broadcasted_iota(jnp.int32, (16, 64), 0)
    token = lax.broadcasted_iota(jnp.int32, (tokens, 64), 0).astype(jnp.float32)
    for out_refs, core in ((other_refs, 1 - place_ref[1]), ((mine_ref,), place_ref[1])):
        total = jnp.zeros(mine_ref.shape, jnp.float32)
        for piece_ref in pieces:
            info = piece_ref[128:, :64].astype(jnp.float32)
            aims = jnp.sum(jnp.where(line == core, info, 0.0), axis=0, keepdims=True)
            matches = jnp.where(aims == token, 1.0, 0.0).astype(jnp.bfloat16)
            at = pl.multiple_of(core * 64, 64)
            total = total + dot_nn(matches, piece_ref[pl.ds(at, 64), :])
        step = tokens // len(out_refs)
        for i, out_ref in enumerate(out_refs):
            out_ref[...] = total[i * step : (i + 1) * step].astype(jnp.bfloat16)


def join_kernel(mine_ref, *refs):
    got_refs, out_ref = refs[:-1], refs[-1]
    step = mine_ref.shape[0] // len(got_refs)
    for i, got_ref in enumerate(got_refs):
        rows = slice(i * step, (i + 1) * step)
        out_ref[rows, :] = mine_ref[rows, :] + got_ref[...]


def halves_of(grad, chips):
    step = grad.shape[1] // (2 * chips)
    return [
        jnp.concatenate([grad[:, (2 * z + c) * step : (2 * z + c + 1) * step] for z in range(chips)], axis=1)
        for c in range(2)
    ]


def split_kernel(chips, place_ref, grad_ref, *refs):
    mine_ref, other_ref = refs[-2:]
    halves = halves_of(grad_ref[...], chips)
    first = place_ref[1] == 0
    half = mine_ref.shape[1]
    mine_ref[...] = jnp.where(first, halves[0], halves[1])
    other_ref[:, :half] = jnp.where(first, halves[1], halves[0])
    if len(refs) == 3:
        other_ref[:, half:] = refs[0][...]


def chip_product_kernel(grad_ref, mixed_ref, got_ref, out_ref):
    half = grad_ref.shape[1]
    total = dot_tn(grad_ref[...], mixed_ref[...]) + dot_tn(got_ref[:, :half], got_ref[:, half:])
    out_ref[...] = total.astype(jnp.bfloat16)


def pack_kernel(time_in, grad_in, grad_got_in, mixed_in, mixed_got_in, packed_out, *scratch):
    time_ref, grad, grad_got, mixed, mixed_got, packed, sems = scratch
    loads = [
        pltpu.make_async_copy(source, target, sems.at[i])
        for i, (source, target) in enumerate(
            ((mixed_in, mixed), (grad_in, grad), (mixed_got_in, mixed_got), (grad_got_in, grad_got), (time_in, time_ref))
        )
    ]
    for load in loads:
        load.start()
    for load in loads:
        load.wait()
    space = dot_tn(grad[...], mixed[...]) + dot_tn(grad_got[...], mixed_got[...])
    time = time_ref[...].astype(jnp.float32)
    main = jnp.concatenate([time[:, :CUT], space[:, :384]], axis=1)
    left = jnp.concatenate([space[:, 384:CUT], time[:, CUT:], space[:, CUT:]], axis=1)
    zero = jnp.zeros((2, 128), jnp.float32)
    blocks, stores = packed.shape[0], []
    for k in range(blocks):
        x = left[k * SHARE : (k + 1) * SHARE, :]
        cut = [x[:, 128 * t : 128 * (t + 1)] for t in range(3)]
        low = [part[5 * u : 5 * u + 5] for part in cut for u in range(2)]
        low.append(jnp.concatenate([part[10:] for part in cut] + [zero], axis=0))
        low.append(jnp.zeros((5, 128), jnp.float32))
        rows = [main[k * SHARE : (k + 1) * SHARE, :], jnp.concatenate(low, axis=1)]
        packed[k] = jnp.concatenate(rows, axis=0).astype(jnp.bfloat16)
        if (k + 1) % 16 == 0:
            at = pl.ds(k - 15, 16)
            stores.append(pltpu.make_async_copy(packed.at[at], packed_out.at[at], sems.at[5 + k // 16]))
            stores[-1].start()
    for store in stores:
        store.wait()


def pack(arrays, blocks):
    scratch = [held(*array.shape) for array in arrays]
    scratch += [held(blocks, 16, 1024), pltpu.SemaphoreType.DMA((5 + blocks // 16,))]
    return call(pack_kernel, bf16(blocks, 16, 1024), arrays, "pack_shares", "aaaaaa", scratch)


def unpack_kernel(parts_ref, space_ref, time_ref):
    total = parts_ref[0].astype(jnp.float32)
    for k in range(1, parts_ref.shape[0]):
        total = total + parts_ref[k].astype(jnp.float32)
    low = [total[SHARE:, 128 * t : 128 * (t + 1)] for t in range(7)]
    left = [
        jnp.concatenate([low[2 * t], low[2 * t + 1], low[6][t : t + 1]], axis=0) for t in range(3)
    ]
    time_ref[...] = jnp.concatenate([total[:SHARE, :CUT], left[2][:, :64]], axis=1)
    space_ref[...] = jnp.concatenate([total[:SHARE, CUT:], left[0], left[1], left[2][:, 64:]], axis=1)


def exchange(tokens, axes):
    devices = lax.axis_size(axes)
    cut = tokens.reshape(devices, tokens.shape[0] // devices, tokens.shape[1])
    return lax.all_to_all(cut, axes, split_axis=0, concat_axis=0, tiled=True).reshape(tokens.shape)


def shift(array, axis, by):
    devices = lax.axis_size(axis)
    return lax.ppermute(array, axis, [(i, (i + by) % devices) for i in range(devices)])


def after(array, *others):
    return lax.optimization_barrier((array, *others))[0]


def body(
    video_tokens, grad_rows, targets, counts, attend_space, output_space, attend_time, output_time
):
    chips = lax.axis_size("z")
    stream = video_tokens[0]
    tokens, width = stream.shape
    place = jnp.stack([lax.axis_index("z"), lax.axis_index("core")]).astype(jnp.int32)

    args = [place, counts, targets, grad_rows.reshape(chips, 128, width)]
    scratch = [pltpu.VMEM(targets.shape, jnp.int32), pltpu.SemaphoreType.DMA((chips + 1,))]
    pieces = call(aim_kernel, [bf16(144, width)] * chips, args, "aim_rows", "ssaa" + "v" * chips, scratch, room=60)
    pieces = [piece if d == 0 else shift(piece, "z", d) for d, piece in enumerate(pieces)]

    space_saved = forward(stream, attend_space, output_space)
    hidden = exchange(space_saved[3], CLIP)

    place = after(place, space_saved[3])
    args = [place, *pieces]
    cuts = 2
    outs = [bf16(tokens, width)] + [bf16(tokens // cuts, width)] * cuts
    mine, *others = call(
        lambda *refs: scatter_kernel(chips, *refs), outs, args, "scatter_rows", "s" + "v" * (chips + 1 + cuts)
    )
    args = [mine] + [shift(other, "core", 1) for other in others]
    grad_out = call(join_kernel, bf16(tokens, width), args, "join_rows", "v" * (cuts + 2))
    grad = exchange(grad_out, CLIP)
    time_saved = forward(hidden, attend_time)
    space_mixed_got = shift(space_saved[2], "core", 1)
    grad_hidden = backward(
        grad, hidden, time_saved[0], time_saved[1], attend_time, output_time, "time_backward"
    )
    time_halves = [bf16(tokens, width // 2), bf16(tokens, width)]
    time_mine, time_other = call(
        lambda *refs: split_kernel(chips, *refs),
        time_halves,
        [after(place, grad_hidden), grad, time_saved[2]],
        "time_split",
        "svvvv",
    )
    time_got = shift(time_other, "core", 1)
    args = [time_mine, time_saved[2], time_got]
    time_sum = call(chip_product_kernel, bf16(width // 2, WIDE), args, "time_weight", "vvvv")

    grad_hidden = exchange(grad_hidden, CLIP)
    half = bf16(tokens, width // 2)
    space_mine, space_other = call(
        lambda *refs: split_kernel(chips, *refs),
        [half, half],
        [after(place, time_sum), grad_hidden],
        "space_split",
        "svvv",
    )
    space_got = shift(space_other, "core", 1)
    packed = pack(
        [time_sum, space_mine, space_got, space_saved[2], space_mixed_got],
        lax.axis_size(("z", "space")),
    )
    packed = lax.all_to_all(packed, ("z", "space"), split_axis=0, concat_axis=0, tiled=True)
    share = jax.ShapeDtypeStruct((SHARE, WIDE), jnp.float32)
    space_grad, time_grad = call(unpack_kernel, [share, share], [packed], "sum_shares", "vvv")
    token_grad = backward(
        grad_hidden, stream, space_saved[0], space_saved[1], attend_space, output_space, "space_backward"
    )
    return (token_grad[None], space_grad, time_grad)


def solution(mesh):
    chips = mesh.shape["tm"] // 2
    fine = Mesh(mesh.devices.reshape(chips, 2, mesh.shape["space"]), ("z", "core", "space"))
    whole = ("z", "core", "space")
    in_specs = (
        P(whole, None, None),
        P(OWNERS, "space", None, None, None),
        P(OWNERS, "space", None, None),
        P(OWNERS, "space", None),
        P(),
        P(),
        P(),
        P(),
    )
    out_specs = (P(whole, None, None), P(whole, None), P(whole, None))
    return jax.shard_map(body, mesh=fine, in_specs=in_specs, out_specs=out_specs, check_vma=False)
```

```python
import jax
import jax.numpy as jnp
from jax import lax
from jax.experimental import pallas as pl
from jax.experimental.pallas import tpu as pltpu
from jax.sharding import Mesh
from jax.sharding import PartitionSpec as P

HEADS = 8
HEAD = 88
WIDE = HEADS * HEAD
EPS = 1e-05
PATCHES = 8
SHARE = 11
CUT = 640
CLIP = ("core", "space")
OWNERS = ("z", "core")
ATTEND_CUTS = ((0, 768), (768, 1344))
VMEM = pl.BlockSpec(memory_space=pltpu.VMEM)
SMEM = pl.BlockSpec(memory_space=pltpu.SMEM)
ANY = pl.BlockSpec(memory_space=pl.ANY)


def bf16(*shape):
    return jax.ShapeDtypeStruct(shape, jnp.bfloat16)


def held(*shape):
    return pltpu.VMEM(shape, jnp.bfloat16)


def call(kernel, outs, args, name, spaces, scratch=(), flops=1e6, room=20):
    spec = {"s": SMEM, "v": VMEM, "a": ANY}
    spaces = [spec[c] for c in spaces]
    many = isinstance(outs, list)
    return pl.pallas_call(
        kernel,
        out_shape=outs,
        in_specs=spaces[: len(args)],
        out_specs=spaces[len(args) :] if many else spaces[-1],
        scratch_shapes=scratch,
        compiler_params=pltpu.CompilerParams(vmem_limit_bytes=room * 2**20),
        cost_estimate=pl.CostEstimate(
            flops=int(flops), bytes_accessed=int(flops / 200), transcendentals=0
        ),
        name=name,
    )(*args)


def normalise(stream):
    widened = stream.astype(jnp.float32)
    center = jnp.mean(widened, axis=-1, keepdims=True)
    centered = widened - center
    variance = jnp.mean(centered * centered, axis=-1, keepdims=True)
    scale = lax.rsqrt(variance + EPS)
    return centered * scale, scale


def dot_nt(a, b):
    return lax.dot_general(a, b, (((1,), (1,)), ((), ())), preferred_element_type=jnp.float32)


def dot_tn(a, b):
    return lax.dot_general(a, b, (((0,), (0,)), ((), ())), preferred_element_type=jnp.float32)


def dot_nn(a, b):
    return jnp.dot(a, b, preferred_element_type=jnp.float32)


def same_patch(tokens):
    row = lax.broadcasted_iota(jnp.int32, (tokens, tokens), 0)
    column = lax.broadcasted_iota(jnp.int32, (tokens, tokens), 1)
    return (row % PATCHES) == (column % PATCHES)


def head(projected_ref, part, h):
    at = (part * HEADS + h) * HEAD
    return projected_ref[:, at : at + HEAD]


def forward_kernel(temporal, *refs):
    if temporal:
        stream_in, attend_in, projected_out, probs_out, mixed_out = refs[:5]
        stream, attend, projected, probs, mixed, sems = refs[5:]
    else:
        stream_in, attend_in, output_in, projected_out, probs_out, result_out = refs[:6]
        stream, attend, projected, probs, output, result, sems = refs[6:]
        mixed = result.at[:, pl.ds(stream.shape[1], WIDE)]
    width = stream.shape[1]

    def copy(source, target, at):
        return pltpu.make_async_copy(source, target, sems.at[at])

    load = copy(stream_in.at[:, pl.ds(0, width)] if temporal else stream_in, stream, 0)
    load.start()
    parts = [
        copy(attend_in.at[pl.ds(a, n)], attend.at[pl.ds(a, n)], 1 + i)
        for i, (a, n) in enumerate(ATTEND_CUTS)
    ]
    for part in parts:
        part.start()
    if not temporal:
        load_output = copy(output_in, output, 4)
        load_output.start()
    load.wait()
    normed = normalise(stream[...])[0].astype(jnp.bfloat16)
    for part, (a, n) in zip(parts, ATTEND_CUTS):
        part.wait()
        projected[:, a : a + n] = dot_nt(normed, attend[a : a + n, :]).astype(jnp.bfloat16)
    stores = [copy(projected, projected_out, 5)]
    stores[0].start()
    tokens = stream.shape[0]
    if temporal:
        allowed = same_patch(tokens)
    for h in range(HEADS):
        scores = dot_nt(head(projected, 0, h), head(projected, 1, h)) * HEAD**-0.5
        if temporal:
            scores = jnp.where(allowed, scores, -jnp.inf)
        weights = jnp.exp(scores - jnp.max(scores, axis=-1, keepdims=True))
        chances = (weights / jnp.sum(weights, axis=-1, keepdims=True)).astype(jnp.bfloat16)
        probs[h] = chances
        mixed[:, h * HEAD : (h + 1) * HEAD] = dot_nn(chances, head(projected, 2, h)).astype(
            jnp.bfloat16
        )
    stores.append(copy(probs, probs_out, 7))
    stores[1].start()
    if temporal:
        stores.append(copy(mixed, mixed_out, 6))
    else:
        load_output.wait()
        branch = dot_nn(mixed[...], output[...])
        result[:, :width] = (stream[...].astype(jnp.float32) + branch).astype(jnp.bfloat16)
        stores.append(copy(result, result_out, 6))
    stores[2].start()
    for store in stores:
        store.wait()


def forward(stream, attend, output=None):
    temporal = output is None
    tokens, width = stream.shape[0], attend.shape[0]
    last = (tokens, WIDE) if temporal else (tokens, width + WIDE)
    shapes = [(tokens, 3 * WIDE), (HEADS, tokens, tokens), last]
    outs = [bf16(*shape) for shape in shapes]
    scratch = [held(tokens, width), held(3 * WIDE, width)] + [held(*shape) for shape in shapes]
    args = [stream, attend.T]
    if not temporal:
        args.append(output.T)
        scratch.insert(4, held(WIDE, width))
    scratch.append(pltpu.SemaphoreType.DMA((16,)))
    name = "time_forward" if temporal else "space_forward"
    spaces = "a" * (len(args) + len(outs))
    return call(lambda *refs: forward_kernel(temporal, *refs), outs, args, name, spaces, scratch, 2.2e9, 60)


def backward_kernel(
    grad_in, stream_in, projected_in, probs_in, attend_in, output_in, result_out,
    grad, stream, projected, probs, attend, output, result, dproj, sems,
):
    bf = jnp.bfloat16

    def copy(source, target, at):
        return pltpu.make_async_copy(source, target, sems.at[at])

    load_grad, load_output = copy(grad_in, grad, 0), copy(output_in, output, 1)
    load_projected = copy(projected_in, projected, 2)
    load_probs = copy(probs_in, probs, 7)
    load_attend, load_stream = copy(attend_in, attend, 3), copy(stream_in.at[:, pl.ds(0, stream.shape[1])], stream, 4)
    for load in (load_grad, load_output, load_projected, load_probs, load_attend, load_stream):
        load.start()
    load_grad.wait()
    load_output.wait()
    dmixed = dot_nt(grad[...], output[...]).astype(bf)
    load_projected.wait()
    load_probs.wait()
    for h in range(HEADS):
        chances = probs[h]
        dm = dmixed[:, h * HEAD : (h + 1) * HEAD]
        dprobs = dot_nt(dm, head(projected, 2, h)).astype(bf).astype(jnp.float32)
        wide = chances.astype(jnp.float32)
        scaled = wide * dprobs
        dscores = (scaled - wide * jnp.sum(scaled, axis=-1, keepdims=True)) * HEAD**-0.5
        dscores = dscores.astype(bf)
        for part, value in (
            (0, dot_nn(dscores, head(projected, 1, h))),
            (1, dot_tn(dscores, head(projected, 0, h))),
            (2, dot_tn(chances, dm)),
        ):
            at = (part * HEADS + h) * HEAD
            dproj[:, at : at + HEAD] = value.astype(bf)
    load_attend.wait()
    load_stream.wait()
    tokens = grad.shape[0]
    for i in range(2):
        rows = slice(i * tokens // 2, (i + 1) * tokens // 2)
        dnormed = dot_nn(dproj[rows, :], attend[...]).astype(bf).astype(jnp.float32)
        normed, scale = normalise(stream[rows, :])
        mean_d = jnp.mean(dnormed, axis=-1, keepdims=True)
        mean_dn = jnp.mean(dnormed * normed, axis=-1, keepdims=True)
        inner = scale * (dnormed - mean_d - normed * mean_dn)
        result[rows, :] = (grad[rows, :].astype(jnp.float32) + inner).astype(bf)
    store = copy(result, result_out, 5)
    store.start()
    store.wait()


def backward(grad, stream, projected, probs, attend, output, name, room):
    args = [grad, stream, projected, probs, attend.T, output.T]
    scratch = [held(*arg.shape) for arg in [grad, grad] + args[2:] + [grad, projected]]
    scratch.append(pltpu.SemaphoreType.DMA((16,)))
    return call(backward_kernel, bf16(*grad.shape), args, name, "a" * 7, scratch, 2.6e9, room)


def aim_kernel(counts_ref, targets_in, rows_in, keep_ref, next_ref, last_ref, targets, sems):
    chips = rows_in.shape[0]
    own = lax.axis_index("z")
    far = (own + 2) % chips
    near = ((keep_ref, own), (next_ref, (own + 1) % chips), (last_ref, (own + chips - 1) % chips))
    loads = [pltpu.make_async_copy(targets_in, targets, sems.at[0])]
    for i, (ref, to) in enumerate(near):
        loads.append(pltpu.make_async_copy(rows_in.at[to], ref.at[pl.ds(0, 128)], sems.at[1 + i]))
    for i, ref in enumerate((next_ref, last_ref)):
        source = rows_in.at[far, pl.ds(64 * i, 64)]
        loads.append(pltpu.make_async_copy(source, ref.at[pl.ds(144, 64)], sems.at[4 + i]))
    for load in loads:
        load.start()
    line = lax.broadcasted_iota(jnp.int32, (16, 64), 0)
    slot = lax.broadcasted_iota(jnp.int32, (16, 64), 1)
    loads[0].wait()
    for ref, to, at in [(ref, to, 128) for ref, to in near] + [(next_ref, far, 208), (last_ref, far, 208)]:
        aims = jnp.full((16, 64), -1, jnp.int32)
        for core in range(2):
            valid = (line == core) & (slot < counts_ref[0, 0, 2 * to + core])
            aims = jnp.where(valid, targets[0, 0, pl.ds(2 * to + core, 1), :], aims)
        ref[at : at + 16, :] = jnp.zeros((16, ref.shape[1]), jnp.bfloat16)
        ref[at : at + 16, :64] = aims.astype(jnp.float32).astype(jnp.bfloat16)
    for load in loads[1:]:
        load.wait()


def scatter_kernel(place_ref, keep_ref, next_ref, last_ref, far0_ref, far1_ref, mine_ref, *other_refs):
    tokens = mine_ref.shape[0]
    line = lax.broadcasted_iota(jnp.int32, (16, 64), 0)
    token = lax.broadcasted_iota(jnp.int32, (tokens, 64), 0).astype(jnp.float32)
    for out_refs, core in ((other_refs, 1 - place_ref[1]), ((mine_ref,), place_ref[1])):
        at = pl.multiple_of(core * 64, 64)
        terms = [(ref[128:144, :64], ref[pl.ds(at, 64), :]) for ref in (keep_ref, next_ref, last_ref)]
        terms.append(
            (
                jnp.where(core == 0, far0_ref[64:80, :64], far1_ref[64:80, :64]),
                jnp.where(core == 0, far0_ref[:64, :], far1_ref[:64, :]),
            )
        )
        total = jnp.zeros(mine_ref.shape, jnp.float32)
        for info, rows in terms:
            info = info.astype(jnp.float32)
            aims = jnp.sum(jnp.where(line == core, info, 0.0), axis=0, keepdims=True)
            matches = jnp.where(aims == token, 1.0, 0.0).astype(jnp.bfloat16)
            total = total + dot_nn(matches, rows)
        step = tokens // len(out_refs)
        for i, out_ref in enumerate(out_refs):
            out_ref[...] = total[i * step : (i + 1) * step].astype(jnp.bfloat16)


def join_kernel(mine_ref, *refs):
    got_refs, out_ref = refs[:-1], refs[-1]
    step = mine_ref.shape[0] // len(got_refs)
    for i, got_ref in enumerate(got_refs):
        rows = slice(i * step, (i + 1) * step)
        out_ref[rows, :] = mine_ref[rows, :] + got_ref[...]


def halves_of(grad, chips):
    step = grad.shape[1] // (2 * chips)
    return [
        jnp.concatenate([grad[:, (2 * z + c) * step : (2 * z + c + 1) * step] for z in range(chips)], axis=1)
        for c in range(2)
    ]


def split_kernel(chips, place_ref, *refs):
    first = place_ref[1] == 0
    for grad_ref, mine_ref, other_ref in (refs[:1] + refs[2:4], refs[1:2] + refs[4:6]):
        halves = halves_of(grad_ref[...], chips)
        mine_ref[...] = jnp.where(first, halves[0], halves[1])
        other_ref[...] = jnp.where(first, halves[1], halves[0])


def pack_kernel(*refs):
    packed_out, packed, sems = refs[8:]
    time, space = (
        dot_tn(grad[...], mixed[...]) + dot_tn(grad_got[...], mixed_got[...])
        for grad, mixed, grad_got, mixed_got in (refs[:4], refs[4:8])
    )
    main = jnp.concatenate([time[:, :CUT], space[:, :384]], axis=1)
    left = jnp.concatenate([space[:, 384:CUT], time[:, CUT:], space[:, CUT:]], axis=1)
    zero = jnp.zeros((2, 128), jnp.float32)
    blocks, stores = packed.shape[0], []
    for k in range(blocks):
        x = left[k * SHARE : (k + 1) * SHARE, :]
        cut = [x[:, 128 * t : 128 * (t + 1)] for t in range(3)]
        low = [part[5 * u : 5 * u + 5] for part in cut for u in range(2)]
        low.append(jnp.concatenate([part[10:] for part in cut] + [zero], axis=0))
        low.append(jnp.zeros((5, 128), jnp.float32))
        rows = [main[k * SHARE : (k + 1) * SHARE, :], jnp.concatenate(low, axis=1)]
        packed[k] = jnp.concatenate(rows, axis=0).astype(jnp.bfloat16)
        if (k + 1) % 16 == 0:
            at = pl.ds(k - 15, 16)
            stores.append(pltpu.make_async_copy(packed.at[at], packed_out.at[at], sems.at[k // 16]))
            stores[-1].start()
    for store in stores:
        store.wait()


def pack(arrays, blocks):
    scratch = [held(blocks, 16, 1024), pltpu.SemaphoreType.DMA((blocks // 16,))]
    return call(pack_kernel, bf16(blocks, 16, 1024), arrays, "pack_shares", "vvvvvvvva", scratch)


def unpack_kernel(parts_ref, space_ref, time_ref):
    total = parts_ref[0].astype(jnp.float32)
    for k in range(1, parts_ref.shape[0]):
        total = total + parts_ref[k].astype(jnp.float32)
    low = [total[SHARE:, 128 * t : 128 * (t + 1)] for t in range(7)]
    left = [
        jnp.concatenate([low[2 * t], low[2 * t + 1], low[6][t : t + 1]], axis=0) for t in range(3)
    ]
    time_ref[...] = jnp.concatenate([total[:SHARE, :CUT], left[2][:, :64]], axis=1)
    space_ref[...] = jnp.concatenate([total[:SHARE, CUT:], left[0], left[1], left[2][:, 64:]], axis=1)


def exchange(tokens, axes):
    devices = lax.axis_size(axes)
    cut = tokens.reshape(devices, tokens.shape[0] // devices, tokens.shape[1])
    return lax.all_to_all(cut, axes, split_axis=0, concat_axis=0, tiled=True).reshape(tokens.shape)


def shift(array, axis, by):
    devices = lax.axis_size(axis)
    return lax.ppermute(array, axis, [(i, (i + by) % devices) for i in range(devices)])


def after(array, *others):
    return lax.optimization_barrier((array, *others))[0]


def body(
    video_tokens, grad_rows, targets, counts, attend_space, output_space, attend_time, output_time
):
    chips = lax.axis_size("z")
    stream = video_tokens[0]
    tokens, width = stream.shape
    place = jnp.stack([lax.axis_index("z"), lax.axis_index("core")]).astype(jnp.int32)

    args = [counts, targets, grad_rows.reshape(chips, 128, width)]
    scratch = [pltpu.VMEM(targets.shape, jnp.int32), pltpu.SemaphoreType.DMA((6,))]
    outs = [bf16(144, width), bf16(224, width), bf16(224, width)]
    keep, to_next, to_last = call(aim_kernel, outs, args, "aim_rows", "saavvv", scratch, room=60)
    from_last, from_next = shift(to_next, "z", 1), shift(to_last, "z", chips - 1)
    far = [shift(from_last[144:], "z", 1), shift(from_next[144:], "z", chips - 1)]

    space_saved = forward(stream, attend_space, output_space)
    hidden = exchange(space_saved[2], CLIP)

    place = after(place, space_saved[2])
    args = [place, keep, from_last, from_next, *far]
    cuts = 2
    outs = [bf16(tokens, width)] + [bf16(tokens // cuts, width)] * cuts
    mine, *others = call(scatter_kernel, outs, args, "scatter_rows", "svvvvv" + "v" * (1 + cuts))
    args = [mine] + [shift(other, "core", 1) for other in others]
    grad_out = call(join_kernel, bf16(tokens, width), args, "join_rows", "v" * (cuts + 2))
    grad = exchange(grad_out, CLIP)
    time_saved = forward(hidden, attend_time)
    time_mixed, space_mixed = time_saved[2], hidden[:, width:]
    time_mixed_got, space_mixed_got = shift(time_mixed, "core", 1), shift(space_mixed, "core", 1)
    grad_hidden = backward(
        grad, hidden, time_saved[0], time_saved[1], attend_time, output_time, "time_backward", 60
    )
    half = bf16(tokens, width // 2)
    time_mine, time_other, space_mine, space_other = call(
        lambda *refs: split_kernel(chips, *refs),
        [half] * 4,
        [place, grad, grad_hidden],
        "split_features",
        "svvvvvv",
    )
    args = [time_mine, time_mixed, shift(time_other, "core", 1), time_mixed_got]
    args += [space_mine, space_mixed, shift(space_other, "core", 1), space_mixed_got]
    packed = pack(args, lax.axis_size(("z", "space")))
    grad_hidden = exchange(grad_hidden, CLIP)
    packed = after(packed, grad_hidden)
    packed = lax.all_to_all(packed, ("z", "space"), split_axis=0, concat_axis=0, tiled=True)
    share = jax.ShapeDtypeStruct((SHARE, WIDE), jnp.float32)
    space_grad, time_grad = call(unpack_kernel, [share, share], [packed], "sum_shares", "vvv")
    token_grad = backward(
        grad_hidden, stream, space_saved[0], space_saved[1], attend_space, output_space, "space_backward", 40
    )
    return (token_grad[None], space_grad, time_grad)


def solution(mesh):
    chips = mesh.shape["tm"] // 2
    fine = Mesh(mesh.devices.reshape(chips, 2, mesh.shape["space"]), ("z", "core", "space"))
    whole = ("z", "core", "space")
    in_specs = (
        P(whole, None, None),
        P(OWNERS, "space", None, None, None),
        P(OWNERS, "space", None, None),
        P(OWNERS, "space", None),
        P(),
        P(),
        P(),
        P(),
    )
    out_specs = (P(whole, None, None), P(whole, None), P(whole, None))
    return jax.shard_map(body, mesh=fine, in_specs=in_specs, out_specs=out_specs, check_vma=False)
```

```python
import jax
import jax.numpy as jnp
from jax import lax
from jax.experimental import pallas as pl
from jax.experimental.pallas import tpu as pltpu
from jax.sharding import Mesh
from jax.sharding import PartitionSpec as P

HEADS = 8
HEAD = 88
WIDE = HEADS * HEAD
EPS = 1e-05
PATCHES = 8
SHARE = 11
CUT = 640
CLIP = ("core", "space")
OWNERS = ("z", "core")
ATTEND_CUTS = ((0, 768), (768, 1344))
VMEM = pl.BlockSpec(memory_space=pltpu.VMEM)
SMEM = pl.BlockSpec(memory_space=pltpu.SMEM)
ANY = pl.BlockSpec(memory_space=pl.ANY)


def bf16(*shape):
    return jax.ShapeDtypeStruct(shape, jnp.bfloat16)


def held(*shape):
    return pltpu.VMEM(shape, jnp.bfloat16)


def call(kernel, outs, args, name, spaces, scratch=(), flops=1e6, room=20):
    spec = {"s": SMEM, "v": VMEM, "a": ANY}
    spaces = [spec[c] for c in spaces]
    many = isinstance(outs, list)
    return pl.pallas_call(
        kernel,
        out_shape=outs,
        in_specs=spaces[: len(args)],
        out_specs=spaces[len(args) :] if many else spaces[-1],
        scratch_shapes=scratch,
        compiler_params=pltpu.CompilerParams(vmem_limit_bytes=room * 2**20),
        cost_estimate=pl.CostEstimate(
            flops=int(flops), bytes_accessed=int(flops / 200), transcendentals=0
        ),
        name=name,
    )(*args)


def normalise(stream):
    widened = stream.astype(jnp.float32)
    center = jnp.mean(widened, axis=-1, keepdims=True)
    centered = widened - center
    variance = jnp.mean(centered * centered, axis=-1, keepdims=True)
    scale = lax.rsqrt(variance + EPS)
    return centered * scale, scale


def dot_nt(a, b):
    return lax.dot_general(a, b, (((1,), (1,)), ((), ())), preferred_element_type=jnp.float32)


def dot_tn(a, b):
    return lax.dot_general(a, b, (((0,), (0,)), ((), ())), preferred_element_type=jnp.float32)


def dot_nn(a, b):
    return jnp.dot(a, b, preferred_element_type=jnp.float32)


def same_patch(tokens):
    row = lax.broadcasted_iota(jnp.int32, (tokens, tokens), 0)
    column = lax.broadcasted_iota(jnp.int32, (tokens, tokens), 1)
    return (row % PATCHES) == (column % PATCHES)


def head(projected_ref, part, h):
    at = (part * HEADS + h) * HEAD
    return projected_ref[:, at : at + HEAD]


def forward_kernel(temporal, *refs):
    if temporal:
        stream_in, attend_in, projected_out, probs_out, mixed_out = refs[:5]
        stream, attend, projected, probs, mixed, sems = refs[5:]
    else:
        stream_in, attend_in, output_in, projected_out, probs_out, result_out = refs[:6]
        stream, attend, projected, probs, output, result, sems = refs[6:]
        mixed = result.at[:, pl.ds(stream.shape[1], WIDE)]
    width = stream.shape[1]

    def copy(source, target, at):
        return pltpu.make_async_copy(source, target, sems.at[at])

    load = copy(stream_in.at[:, pl.ds(0, width)] if temporal else stream_in, stream, 0)
    load.start()
    parts = [
        copy(attend_in.at[pl.ds(a, n)], attend.at[pl.ds(a, n)], 1 + i)
        for i, (a, n) in enumerate(ATTEND_CUTS)
    ]
    for part in parts:
        part.start()
    if not temporal:
        load_output = copy(output_in, output, 4)
        load_output.start()
    load.wait()
    normed = normalise(stream[...])[0].astype(jnp.bfloat16)
    for part, (a, n) in zip(parts, ATTEND_CUTS):
        part.wait()
        projected[:, a : a + n] = dot_nt(normed, attend[a : a + n, :]).astype(jnp.bfloat16)
    stores = [copy(projected, projected_out, 5)]
    stores[0].start()
    tokens = stream.shape[0]
    if temporal:
        allowed = same_patch(tokens)
    ahead = dot_nt(head(projected, 0, 0), head(projected, 1, 0))
    for h in range(HEADS):
        scores = ahead * HEAD**-0.5
        if h + 1 < HEADS:
            ahead = dot_nt(head(projected, 0, h + 1), head(projected, 1, h + 1))
        if temporal:
            scores = jnp.where(allowed, scores, -jnp.inf)
        weights = jnp.exp(scores - jnp.max(scores, axis=-1, keepdims=True))
        chances = (weights / jnp.sum(weights, axis=-1, keepdims=True)).astype(jnp.bfloat16)
        probs[h] = chances
        mixed[:, h * HEAD : (h + 1) * HEAD] = dot_nn(chances, head(projected, 2, h)).astype(
            jnp.bfloat16
        )
    stores.append(copy(probs, probs_out, 7))
    stores[1].start()
    if temporal:
        stores.append(copy(mixed, mixed_out, 6))
    else:
        load_output.wait()
        branch = dot_nn(mixed[...], output[...])
        result[:, :width] = (stream[...].astype(jnp.float32) + branch).astype(jnp.bfloat16)
        stores.append(copy(result, result_out, 6))
    stores[2].start()
    for store in stores:
        store.wait()


def forward(stream, attend, output=None):
    temporal = output is None
    tokens, width = stream.shape[0], attend.shape[0]
    last = (tokens, WIDE) if temporal else (tokens, width + WIDE)
    shapes = [(tokens, 3 * WIDE), (HEADS, tokens, tokens), last]
    outs = [bf16(*shape) for shape in shapes]
    scratch = [held(tokens, width), held(3 * WIDE, width)] + [held(*shape) for shape in shapes]
    args = [stream, attend.T]
    if not temporal:
        args.append(output.T)
        scratch.insert(4, held(WIDE, width))
    scratch.append(pltpu.SemaphoreType.DMA((16,)))
    name = "time_forward" if temporal else "space_forward"
    spaces = "a" * (len(args) + len(outs))
    return call(lambda *refs: forward_kernel(temporal, *refs), outs, args, name, spaces, scratch, 2.2e9, 60)


def backward_kernel(
    grad_in, stream_in, projected_in, probs_in, attend_in, output_in, result_out,
    grad, stream, projected, probs, attend, output, result, dproj, sems,
):
    bf = jnp.bfloat16

    def copy(source, target, at):
        return pltpu.make_async_copy(source, target, sems.at[at])

    load_grad, load_output = copy(grad_in, grad, 0), copy(output_in, output, 1)
    load_projected = copy(projected_in, projected, 2)
    load_probs = copy(probs_in, probs, 7)
    load_attend, load_stream = copy(attend_in, attend, 3), copy(stream_in.at[:, pl.ds(0, stream.shape[1])], stream, 4)
    for load in (load_grad, load_output, load_projected, load_probs, load_attend, load_stream):
        load.start()
    load_grad.wait()
    load_output.wait()
    dmixed = dot_nt(grad[...], output[...]).astype(bf)
    load_projected.wait()
    load_probs.wait()
    for h in range(HEADS):
        chances = probs[h]
        dm = dmixed[:, h * HEAD : (h + 1) * HEAD]
        dprobs = dot_nt(dm, head(projected, 2, h)).astype(bf).astype(jnp.float32)
        wide = chances.astype(jnp.float32)
        scaled = wide * dprobs
        dscores = (scaled - wide * jnp.sum(scaled, axis=-1, keepdims=True)) * HEAD**-0.5
        dscores = dscores.astype(bf)
        for part, value in (
            (0, dot_nn(dscores, head(projected, 1, h))),
            (1, dot_tn(dscores, head(projected, 0, h))),
            (2, dot_tn(chances, dm)),
        ):
            at = (part * HEADS + h) * HEAD
            dproj[:, at : at + HEAD] = value.astype(bf)
    load_attend.wait()
    load_stream.wait()
    tokens = grad.shape[0]
    for i in range(2):
        rows = slice(i * tokens // 2, (i + 1) * tokens // 2)
        dnormed = dot_nn(dproj[rows, :], attend[...]).astype(bf).astype(jnp.float32)
        normed, scale = normalise(stream[rows, :])
        mean_d = jnp.mean(dnormed, axis=-1, keepdims=True)
        mean_dn = jnp.mean(dnormed * normed, axis=-1, keepdims=True)
        inner = scale * (dnormed - mean_d - normed * mean_dn)
        result[rows, :] = (grad[rows, :].astype(jnp.float32) + inner).astype(bf)
    store = copy(result, result_out, 5)
    store.start()
    store.wait()


def backward(grad, stream, projected, probs, attend, output, name, room):
    args = [grad, stream, projected, probs, attend.T, output.T]
    scratch = [held(*arg.shape) for arg in [grad, grad] + args[2:] + [grad, projected]]
    scratch.append(pltpu.SemaphoreType.DMA((16,)))
    return call(backward_kernel, bf16(*grad.shape), args, name, "a" * 7, scratch, 2.6e9, room)


def aim_kernel(counts_ref, targets_in, rows_in, keep_ref, next_ref, last_ref, targets, sems):
    chips = rows_in.shape[0]
    own = lax.axis_index("z")
    far = (own + 2) % chips
    near = ((keep_ref, own), (next_ref, (own + 1) % chips), (last_ref, (own + chips - 1) % chips))
    loads = [pltpu.make_async_copy(targets_in, targets, sems.at[0])]
    for i, (ref, to) in enumerate(near):
        loads.append(pltpu.make_async_copy(rows_in.at[to], ref.at[pl.ds(0, 128)], sems.at[1 + i]))
    for i, ref in enumerate((next_ref, last_ref)):
        source = rows_in.at[far, pl.ds(64 * i, 64)]
        loads.append(pltpu.make_async_copy(source, ref.at[pl.ds(144, 64)], sems.at[4 + i]))
    for load in loads:
        load.start()
    line = lax.broadcasted_iota(jnp.int32, (16, 64), 0)
    slot = lax.broadcasted_iota(jnp.int32, (16, 64), 1)
    loads[0].wait()
    for ref, to, at in [(ref, to, 128) for ref, to in near] + [(next_ref, far, 208), (last_ref, far, 208)]:
        aims = jnp.full((16, 64), -1, jnp.int32)
        for core in range(2):
            valid = (line == core) & (slot < counts_ref[0, 0, 2 * to + core])
            aims = jnp.where(valid, targets[0, 0, pl.ds(2 * to + core, 1), :], aims)
        ref[at : at + 16, :] = jnp.zeros((16, ref.shape[1]), jnp.bfloat16)
        ref[at : at + 16, :64] = aims.astype(jnp.float32).astype(jnp.bfloat16)
    for load in loads[1:]:
        load.wait()


def scatter_kernel(place_ref, keep_ref, next_ref, last_ref, far0_ref, far1_ref, mine_ref, *other_refs):
    tokens = mine_ref.shape[0]
    line = lax.broadcasted_iota(jnp.int32, (16, 64), 0)
    token = lax.broadcasted_iota(jnp.int32, (tokens, 64), 0).astype(jnp.float32)
    for out_refs, core in ((other_refs, 1 - place_ref[1]), ((mine_ref,), place_ref[1])):
        at = pl.multiple_of(core * 64, 64)
        terms = [(ref[128:144, :64], ref[pl.ds(at, 64), :]) for ref in (keep_ref, next_ref, last_ref)]
        terms.append(
            (
                jnp.where(core == 0, far0_ref[64:80, :64], far1_ref[64:80, :64]),
                jnp.where(core == 0, far0_ref[:64, :], far1_ref[:64, :]),
            )
        )
        total = jnp.zeros(mine_ref.shape, jnp.float32)
        for info, rows in terms:
            info = info.astype(jnp.float32)
            aims = jnp.sum(jnp.where(line == core, info, 0.0), axis=0, keepdims=True)
            matches = jnp.where(aims == token, 1.0, 0.0).astype(jnp.bfloat16)
            total = total + dot_nn(matches, rows)
        step = tokens // len(out_refs)
        for i, out_ref in enumerate(out_refs):
            out_ref[...] = total[i * step : (i + 1) * step].astype(jnp.bfloat16)


def join_kernel(mine_ref, *refs):
    got_refs, out_ref = refs[:-1], refs[-1]
    step = mine_ref.shape[0] // len(got_refs)
    for i, got_ref in enumerate(got_refs):
        rows = slice(i * step, (i + 1) * step)
        out_ref[rows, :] = mine_ref[rows, :] + got_ref[...]


def halves_of(grad, chips):
    step = grad.shape[1] // (2 * chips)
    return [
        jnp.concatenate([grad[:, (2 * z + c) * step : (2 * z + c + 1) * step] for z in range(chips)], axis=1)
        for c in range(2)
    ]


def split_kernel(chips, place_ref, *refs):
    first = place_ref[1] == 0
    for grad_ref, mine_ref, other_ref in (refs[:1] + refs[2:4], refs[1:2] + refs[4:6]):
        halves = halves_of(grad_ref[...], chips)
        mine_ref[...] = jnp.where(first, halves[0], halves[1])
        other_ref[...] = jnp.where(first, halves[1], halves[0])


def pack_kernel(*refs):
    packed_out, packed, sems = refs[8:]
    time, space = (
        dot_tn(grad[...], mixed[...]) + dot_tn(grad_got[...], mixed_got[...])
        for grad, mixed, grad_got, mixed_got in (refs[:4], refs[4:8])
    )
    main = jnp.concatenate([time[:, :CUT], space[:, :384]], axis=1)
    left = jnp.concatenate([space[:, 384:CUT], time[:, CUT:], space[:, CUT:]], axis=1)
    zero = jnp.zeros((2, 128), jnp.float32)
    blocks, stores = packed.shape[0], []
    for k in range(blocks):
        x = left[k * SHARE : (k + 1) * SHARE, :]
        cut = [x[:, 128 * t : 128 * (t + 1)] for t in range(3)]
        low = [part[5 * u : 5 * u + 5] for part in cut for u in range(2)]
        low.append(jnp.concatenate([part[10:] for part in cut] + [zero], axis=0))
        low.append(jnp.zeros((5, 128), jnp.float32))
        rows = [main[k * SHARE : (k + 1) * SHARE, :], jnp.concatenate(low, axis=1)]
        packed[k] = jnp.concatenate(rows, axis=0).astype(jnp.bfloat16)
        if (k + 1) % 16 == 0:
            at = pl.ds(k - 15, 16)
            stores.append(pltpu.make_async_copy(packed.at[at], packed_out.at[at], sems.at[k // 16]))
            stores[-1].start()
    for store in stores:
        store.wait()


def pack(arrays, blocks):
    scratch = [held(blocks, 16, 1024), pltpu.SemaphoreType.DMA((blocks // 16,))]
    return call(pack_kernel, bf16(blocks, 16, 1024), arrays, "pack_shares", "vvvvvvvva", scratch)


def unpack_kernel(parts_ref, space_ref, time_ref):
    total = parts_ref[0].astype(jnp.float32)
    for k in range(1, parts_ref.shape[0]):
        total = total + parts_ref[k].astype(jnp.float32)
    low = [total[SHARE:, 128 * t : 128 * (t + 1)] for t in range(7)]
    left = [
        jnp.concatenate([low[2 * t], low[2 * t + 1], low[6][t : t + 1]], axis=0) for t in range(3)
    ]
    time_ref[...] = jnp.concatenate([total[:SHARE, :CUT], left[2][:, :64]], axis=1)
    space_ref[...] = jnp.concatenate([total[:SHARE, CUT:], left[0], left[1], left[2][:, 64:]], axis=1)


def exchange(tokens, axes):
    devices = lax.axis_size(axes)
    cut = tokens.reshape(devices, tokens.shape[0] // devices, tokens.shape[1])
    return lax.all_to_all(cut, axes, split_axis=0, concat_axis=0, tiled=True).reshape(tokens.shape)


def shift(array, axis, by):
    devices = lax.axis_size(axis)
    return lax.ppermute(array, axis, [(i, (i + by) % devices) for i in range(devices)])


def after(array, *others):
    return lax.optimization_barrier((array, *others))[0]


def body(
    video_tokens, grad_rows, targets, counts, attend_space, output_space, attend_time, output_time
):
    chips = lax.axis_size("z")
    stream = video_tokens[0]
    tokens, width = stream.shape
    place = jnp.stack([lax.axis_index("z"), lax.axis_index("core")]).astype(jnp.int32)

    args = [counts, targets, grad_rows.reshape(chips, 128, width)]
    scratch = [pltpu.VMEM(targets.shape, jnp.int32), pltpu.SemaphoreType.DMA((6,))]
    outs = [bf16(144, width), bf16(224, width), bf16(224, width)]
    keep, to_next, to_last = call(aim_kernel, outs, args, "aim_rows", "saavvv", scratch, room=60)
    from_last, from_next = shift(to_next, "z", 1), shift(to_last, "z", chips - 1)
    far = [shift(from_last[144:], "z", 1), shift(from_next[144:], "z", chips - 1)]

    space_saved = forward(stream, attend_space, output_space)
    hidden = exchange(space_saved[2], CLIP)

    place = after(place, space_saved[2])
    args = [place, keep, from_last, from_next, *far]
    cuts = 2
    outs = [bf16(tokens, width)] + [bf16(tokens // cuts, width)] * cuts
    mine, *others = call(scatter_kernel, outs, args, "scatter_rows", "svvvvv" + "v" * (1 + cuts))
    args = [mine] + [shift(other, "core", 1) for other in others]
    grad_out = call(join_kernel, bf16(tokens, width), args, "join_rows", "v" * (cuts + 2))
    grad = exchange(grad_out, CLIP)
    time_saved = forward(hidden, attend_time)
    time_mixed, space_mixed = time_saved[2], hidden[:, width:]
    time_mixed_got, space_mixed_got = shift(time_mixed, "core", 1), shift(space_mixed, "core", 1)
    grad_hidden = backward(
        grad, hidden, time_saved[0], time_saved[1], attend_time, output_time, "time_backward", 60
    )
    half = bf16(tokens, width // 2)
    time_mine, time_other, space_mine, space_other = call(
        lambda *refs: split_kernel(chips, *refs),
        [half] * 4,
        [place, grad, grad_hidden],
        "split_features",
        "svvvvvv",
    )
    args = [time_mine, time_mixed, shift(time_other, "core", 1), time_mixed_got]
    args += [space_mine, space_mixed, shift(space_other, "core", 1), space_mixed_got]
    packed = pack(args, lax.axis_size(("z", "space")))
    grad_hidden = exchange(grad_hidden, CLIP)
    packed = after(packed, grad_hidden)
    packed = lax.all_to_all(packed, ("z", "space"), split_axis=0, concat_axis=0, tiled=True)
    share = jax.ShapeDtypeStruct((SHARE, WIDE), jnp.float32)
    space_grad, time_grad = call(unpack_kernel, [share, share], [packed], "sum_shares", "vvv")
    token_grad = backward(
        grad_hidden, stream, space_saved[0], space_saved[1], attend_space, output_space, "space_backward", 40
    )
    return (token_grad[None], space_grad, time_grad)


def solution(mesh):
    chips = mesh.shape["tm"] // 2
    fine = Mesh(mesh.devices.reshape(chips, 2, mesh.shape["space"]), ("z", "core", "space"))
    whole = ("z", "core", "space")
    in_specs = (
        P(whole, None, None),
        P(OWNERS, "space", None, None, None),
        P(OWNERS, "space", None, None),
        P(OWNERS, "space", None),
        P(),
        P(),
        P(),
        P(),
    )
    out_specs = (P(whole, None, None), P(whole, None), P(whole, None))
    return jax.shard_map(body, mesh=fine, in_specs=in_specs, out_specs=out_specs, check_vma=False)
```

```python
import jax
import jax.numpy as jnp
from jax import lax
from jax.experimental import pallas as pl
from jax.experimental.pallas import tpu as pltpu
from jax.sharding import Mesh
from jax.sharding import PartitionSpec as P

HEADS = 8
HEAD = 88
WIDE = HEADS * HEAD
EPS = 1e-05
PATCHES = 8
SHARE = 11
CUT = 640
CLIP = ("core", "space")
OWNERS = ("z", "core")
ATTEND_CUTS = ((0, 768), (768, 1344))
VMEM = pl.BlockSpec(memory_space=pltpu.VMEM)
SMEM = pl.BlockSpec(memory_space=pltpu.SMEM)
ANY = pl.BlockSpec(memory_space=pl.ANY)


def bf16(*shape):
    return jax.ShapeDtypeStruct(shape, jnp.bfloat16)


def held(*shape):
    return pltpu.VMEM(shape, jnp.bfloat16)


def call(kernel, outs, args, name, spaces, scratch=(), flops=1e6, room=20):
    spec = {"s": SMEM, "v": VMEM, "a": ANY}
    spaces = [spec[c] for c in spaces]
    many = isinstance(outs, list)
    return pl.pallas_call(
        kernel,
        out_shape=outs,
        in_specs=spaces[: len(args)],
        out_specs=spaces[len(args) :] if many else spaces[-1],
        scratch_shapes=scratch,
        compiler_params=pltpu.CompilerParams(vmem_limit_bytes=room * 2**20),
        cost_estimate=pl.CostEstimate(
            flops=int(flops), bytes_accessed=int(flops / 200), transcendentals=0
        ),
        name=name,
    )(*args)


def normalise(stream):
    widened = stream.astype(jnp.float32)
    center = jnp.mean(widened, axis=-1, keepdims=True)
    centered = widened - center
    variance = jnp.mean(centered * centered, axis=-1, keepdims=True)
    scale = lax.rsqrt(variance + EPS)
    return centered * scale, scale


def dot_nt(a, b):
    return lax.dot_general(a, b, (((1,), (1,)), ((), ())), preferred_element_type=jnp.float32)


def dot_tn(a, b):
    return lax.dot_general(a, b, (((0,), (0,)), ((), ())), preferred_element_type=jnp.float32)


def dot_nn(a, b):
    return jnp.dot(a, b, preferred_element_type=jnp.float32)


def same_patch(tokens):
    row = lax.broadcasted_iota(jnp.int32, (tokens, tokens), 0)
    column = lax.broadcasted_iota(jnp.int32, (tokens, tokens), 1)
    return (row % PATCHES) == (column % PATCHES)


def head(projected_ref, part, h):
    at = (part * HEADS + h) * HEAD
    return projected_ref[:, at : at + HEAD]


def forward_kernel(temporal, *refs):
    if temporal:
        stream_in, attend_in, projected_out, probs_out, mixed_out = refs[:5]
        stream, attend, projected, probs, mixed, sems = refs[5:]
    else:
        stream_in, attend_in, output_in, projected_out, probs_out, result_out = refs[:6]
        stream, attend, projected, probs, output, result, sems = refs[6:]
        mixed = result.at[:, pl.ds(stream.shape[1], WIDE)]
    width = stream.shape[1]

    def copy(source, target, at):
        return pltpu.make_async_copy(source, target, sems.at[at])

    load = copy(stream_in.at[:, pl.ds(0, width)] if temporal else stream_in, stream, 0)
    load.start()
    parts = [
        copy(attend_in.at[pl.ds(a, n)], attend.at[pl.ds(a, n)], 1 + i)
        for i, (a, n) in enumerate(ATTEND_CUTS)
    ]
    for part in parts:
        part.start()
    if not temporal:
        load_output = copy(output_in, output, 4)
        load_output.start()
    load.wait()
    normed = normalise(stream[...])[0].astype(jnp.bfloat16)
    for part, (a, n) in zip(parts, ATTEND_CUTS):
        part.wait()
        projected[:, a : a + n] = dot_nt(normed, attend[a : a + n, :]).astype(jnp.bfloat16)
    stores = [copy(projected, projected_out, 5)]
    stores[0].start()
    tokens = stream.shape[0]
    if temporal:
        allowed = same_patch(tokens)
    ahead = dot_nt(head(projected, 0, 0), head(projected, 1, 0))
    for h in range(HEADS):
        scores = ahead * HEAD**-0.5
        if h + 1 < HEADS:
            ahead = dot_nt(head(projected, 0, h + 1), head(projected, 1, h + 1))
        if temporal:
            scores = jnp.where(allowed, scores, -jnp.inf)
        weights = jnp.exp(scores - jnp.max(scores, axis=-1, keepdims=True))
        chances = (weights / jnp.sum(weights, axis=-1, keepdims=True)).astype(jnp.bfloat16)
        probs[h] = chances
        mixed[:, h * HEAD : (h + 1) * HEAD] = dot_nn(chances, head(projected, 2, h)).astype(
            jnp.bfloat16
        )
    stores.append(copy(probs, probs_out, 7))
    stores[1].start()
    if temporal:
        stores.append(copy(mixed, mixed_out, 6))
    else:
        load_output.wait()
        branch = dot_nn(mixed[...], output[...])
        result[:, :width] = (stream[...].astype(jnp.float32) + branch).astype(jnp.bfloat16)
        stores.append(copy(result, result_out, 6))
    stores[2].start()
    for store in stores:
        store.wait()


def forward(stream, attend, output=None):
    temporal = output is None
    tokens, width = stream.shape[0], attend.shape[0]
    last = (tokens, WIDE) if temporal else (tokens, width + WIDE)
    shapes = [(tokens, 3 * WIDE), (HEADS, tokens, tokens), last]
    outs = [bf16(*shape) for shape in shapes]
    scratch = [held(tokens, width), held(3 * WIDE, width)] + [held(*shape) for shape in shapes]
    args = [stream, attend.T]
    if not temporal:
        args.append(output.T)
        scratch.insert(4, held(WIDE, width))
    scratch.append(pltpu.SemaphoreType.DMA((16,)))
    name = "time_forward" if temporal else "space_forward"
    spaces = "a" * (len(args) + len(outs))
    return call(lambda *refs: forward_kernel(temporal, *refs), outs, args, name, spaces, scratch, 2.2e9, 60)


def backward_kernel(
    grad_in, stream_in, projected_in, probs_in, attend_in, output_in, result_out,
    grad, stream, projected, probs, attend, output, result, dproj, sems,
):
    bf = jnp.bfloat16

    def copy(source, target, at):
        return pltpu.make_async_copy(source, target, sems.at[at])

    load_grad, load_output = copy(grad_in, grad, 0), copy(output_in, output, 1)
    load_projected = copy(projected_in, projected, 2)
    load_probs = copy(probs_in, probs, 7)
    load_attend, load_stream = copy(attend_in, attend, 3), copy(stream_in.at[:, pl.ds(0, stream.shape[1])], stream, 4)
    for load in (load_grad, load_output, load_projected, load_probs, load_attend, load_stream):
        load.start()
    load_grad.wait()
    load_output.wait()
    dmixed = dot_nt(grad[...], output[...]).astype(bf)
    load_projected.wait()
    load_probs.wait()
    for h in range(HEADS):
        chances = probs[h]
        dm = dmixed[:, h * HEAD : (h + 1) * HEAD]
        dprobs = dot_nt(dm, head(projected, 2, h)).astype(bf).astype(jnp.float32)
        wide = chances.astype(jnp.float32)
        scaled = wide * dprobs
        dscores = (scaled - wide * jnp.sum(scaled, axis=-1, keepdims=True)) * HEAD**-0.5
        dscores = dscores.astype(bf)
        for part, value in (
            (0, dot_nn(dscores, head(projected, 1, h))),
            (1, dot_tn(dscores, head(projected, 0, h))),
            (2, dot_tn(chances, dm)),
        ):
            at = (part * HEADS + h) * HEAD
            dproj[:, at : at + HEAD] = value.astype(bf)
    load_attend.wait()
    load_stream.wait()
    tokens = grad.shape[0]
    for i in range(2):
        rows = slice(i * tokens // 2, (i + 1) * tokens // 2)
        dnormed = dot_nn(dproj[rows, :], attend[...]).astype(bf).astype(jnp.float32)
        normed, scale = normalise(stream[rows, :])
        mean_d = jnp.mean(dnormed, axis=-1, keepdims=True)
        mean_dn = jnp.mean(dnormed * normed, axis=-1, keepdims=True)
        inner = scale * (dnormed - mean_d - normed * mean_dn)
        result[rows, :] = (grad[rows, :].astype(jnp.float32) + inner).astype(bf)
    store = copy(result, result_out, 5)
    store.start()
    store.wait()


def backward(grad, stream, projected, probs, attend, output, name, room):
    args = [grad, stream, projected, probs, attend.T, output.T]
    scratch = [held(*arg.shape) for arg in [grad, grad] + args[2:] + [grad, projected]]
    scratch.append(pltpu.SemaphoreType.DMA((16,)))
    return call(backward_kernel, bf16(*grad.shape), args, name, "a" * 7, scratch, 2.6e9, room)


def put_targets(counts_ref, targets, ref, to, at):
    line = lax.broadcasted_iota(jnp.int32, (16, 64), 0)
    slot = lax.broadcasted_iota(jnp.int32, (16, 64), 1)
    aims = jnp.full((16, 64), -1, jnp.int32)
    for core in range(2):
        valid = (line == core) & (slot < counts_ref[0, 0, 2 * to + core])
        aims = jnp.where(valid, targets[0, 0, pl.ds(2 * to + core, 1), :], aims)
    ref[at : at + 16, :] = jnp.zeros((16, ref.shape[1]), jnp.bfloat16)
    ref[at : at + 16, :64] = aims.astype(jnp.float32).astype(jnp.bfloat16)


def aim_kernel(counts_ref, targets_in, rows_in, next_ref, last_ref, targets, sems):
    chips = rows_in.shape[0]
    own = lax.axis_index("z")
    far = (own + 2) % chips
    near = ((next_ref, (own + 1) % chips), (last_ref, (own + chips - 1) % chips))
    loads = [pltpu.make_async_copy(targets_in, targets, sems.at[0])]
    for i, (ref, to) in enumerate(near):
        loads.append(pltpu.make_async_copy(rows_in.at[to], ref.at[pl.ds(0, 128)], sems.at[1 + i]))
        source = rows_in.at[far, pl.ds(64 * i, 64)]
        loads.append(pltpu.make_async_copy(source, ref.at[pl.ds(144, 64)], sems.at[3 + i]))
    for load in loads:
        load.start()
    loads[0].wait()
    for ref, to in near:
        put_targets(counts_ref, targets, ref, to, 128)
        put_targets(counts_ref, targets, ref, far, 208)
    for load in loads[1:]:
        load.wait()


def keep_kernel(counts_ref, targets_in, rows_in, keep_ref, targets, sems):
    own = lax.axis_index("z")
    loads = [
        pltpu.make_async_copy(targets_in, targets, sems.at[0]),
        pltpu.make_async_copy(rows_in.at[own], keep_ref.at[pl.ds(0, 128)], sems.at[1]),
    ]
    for load in loads:
        load.start()
    loads[0].wait()
    put_targets(counts_ref, targets, keep_ref, own, 128)
    loads[1].wait()


def scatter_kernel(place_ref, keep_ref, next_ref, last_ref, far0_ref, far1_ref, mine_ref, *other_refs):
    tokens = mine_ref.shape[0]
    line = lax.broadcasted_iota(jnp.int32, (16, 64), 0)
    token = lax.broadcasted_iota(jnp.int32, (tokens, 64), 0).astype(jnp.float32)
    for out_refs, core in ((other_refs, 1 - place_ref[1]), ((mine_ref,), place_ref[1])):
        at = pl.multiple_of(core * 64, 64)
        terms = [(ref[128:144, :64], ref[pl.ds(at, 64), :]) for ref in (keep_ref, next_ref, last_ref)]
        terms.append(
            (
                jnp.where(core == 0, far0_ref[64:80, :64], far1_ref[64:80, :64]),
                jnp.where(core == 0, far0_ref[:64, :], far1_ref[:64, :]),
            )
        )
        total = jnp.zeros(mine_ref.shape, jnp.float32)
        for info, rows in terms:
            info = info.astype(jnp.float32)
            aims = jnp.sum(jnp.where(line == core, info, 0.0), axis=0, keepdims=True)
            matches = jnp.where(aims == token, 1.0, 0.0).astype(jnp.bfloat16)
            total = total + dot_nn(matches, rows)
        step = tokens // len(out_refs)
        for i, out_ref in enumerate(out_refs):
            out_ref[...] = total[i * step : (i + 1) * step].astype(jnp.bfloat16)


def join_kernel(mine_ref, *refs):
    got_refs, out_ref = refs[:-1], refs[-1]
    step = mine_ref.shape[0] // len(got_refs)
    for i, got_ref in enumerate(got_refs):
        rows = slice(i * step, (i + 1) * step)
        out_ref[rows, :] = mine_ref[rows, :] + got_ref[...]


def halves_of(grad, chips):
    step = grad.shape[1] // (2 * chips)
    return [
        jnp.concatenate([grad[:, (2 * z + c) * step : (2 * z + c + 1) * step] for z in range(chips)], axis=1)
        for c in range(2)
    ]


def split_kernel(chips, place_ref, *refs):
    first = place_ref[1] == 0
    for grad_ref, mine_ref, other_ref in (refs[:1] + refs[2:4], refs[1:2] + refs[4:6]):
        halves = halves_of(grad_ref[...], chips)
        mine_ref[...] = jnp.where(first, halves[0], halves[1])
        other_ref[...] = jnp.where(first, halves[1], halves[0])


def pack_kernel(*refs):
    packed_out, packed, sems = refs[8:]
    time, space = (
        dot_tn(grad[...], mixed[...]) + dot_tn(grad_got[...], mixed_got[...])
        for grad, mixed, grad_got, mixed_got in (refs[:4], refs[4:8])
    )
    main = jnp.concatenate([time[:, :CUT], space[:, :384]], axis=1)
    left = jnp.concatenate([space[:, 384:CUT], time[:, CUT:], space[:, CUT:]], axis=1)
    zero = jnp.zeros((2, 128), jnp.float32)
    blocks, stores = packed.shape[0], []
    for k in range(blocks):
        x = left[k * SHARE : (k + 1) * SHARE, :]
        cut = [x[:, 128 * t : 128 * (t + 1)] for t in range(3)]
        low = [part[5 * u : 5 * u + 5] for part in cut for u in range(2)]
        low.append(jnp.concatenate([part[10:] for part in cut] + [zero], axis=0))
        low.append(jnp.zeros((5, 128), jnp.float32))
        rows = [main[k * SHARE : (k + 1) * SHARE, :], jnp.concatenate(low, axis=1)]
        packed[k] = jnp.concatenate(rows, axis=0).astype(jnp.bfloat16)
        if (k + 1) % 16 == 0:
            at = pl.ds(k - 15, 16)
            stores.append(pltpu.make_async_copy(packed.at[at], packed_out.at[at], sems.at[k // 16]))
            stores[-1].start()
    for store in stores:
        store.wait()


def pack(arrays, blocks):
    scratch = [held(blocks, 16, 1024), pltpu.SemaphoreType.DMA((blocks // 16,))]
    return call(pack_kernel, bf16(blocks, 16, 1024), arrays, "pack_shares", "vvvvvvvva", scratch)


def unpack_kernel(parts_ref, space_ref, time_ref):
    total = parts_ref[0].astype(jnp.float32)
    for k in range(1, parts_ref.shape[0]):
        total = total + parts_ref[k].astype(jnp.float32)
    low = [total[SHARE:, 128 * t : 128 * (t + 1)] for t in range(7)]
    left = [
        jnp.concatenate([low[2 * t], low[2 * t + 1], low[6][t : t + 1]], axis=0) for t in range(3)
    ]
    time_ref[...] = jnp.concatenate([total[:SHARE, :CUT], left[2][:, :64]], axis=1)
    space_ref[...] = jnp.concatenate([total[:SHARE, CUT:], left[0], left[1], left[2][:, 64:]], axis=1)


def exchange(tokens, axes):
    devices = lax.axis_size(axes)
    cut = tokens.reshape(devices, tokens.shape[0] // devices, tokens.shape[1])
    return lax.all_to_all(cut, axes, split_axis=0, concat_axis=0, tiled=True).reshape(tokens.shape)


def shift(array, axis, by):
    devices = lax.axis_size(axis)
    return lax.ppermute(array, axis, [(i, (i + by) % devices) for i in range(devices)])


def after(array, *others):
    return lax.optimization_barrier((array, *others))[0]


def body(
    video_tokens, grad_rows, targets, counts, attend_space, output_space, attend_time, output_time
):
    chips = lax.axis_size("z")
    stream = video_tokens[0]
    tokens, width = stream.shape
    place = jnp.stack([lax.axis_index("z"), lax.axis_index("core")]).astype(jnp.int32)

    args = [counts, targets, grad_rows.reshape(chips, 128, width)]
    scratch = [pltpu.VMEM(targets.shape, jnp.int32), pltpu.SemaphoreType.DMA((6,))]
    outs = [bf16(224, width), bf16(224, width)]
    to_next, to_last = call(aim_kernel, outs, args, "aim_rows", "saavv", scratch, room=60)
    from_last, from_next = shift(to_next, "z", 1), shift(to_last, "z", chips - 1)
    far = [shift(from_last[144:], "z", 1), shift(from_next[144:], "z", chips - 1)]

    space_saved = forward(stream, attend_space, output_space)
    hidden = exchange(space_saved[2], CLIP)

    place = after(place, space_saved[2])
    keep_args = [after(counts, space_saved[2])] + args[1:]
    keep = call(keep_kernel, bf16(144, width), keep_args, "keep_rows", "saav", scratch, room=60)
    args = [place, keep, from_last, from_next, *far]
    cuts = 2
    outs = [bf16(tokens, width)] + [bf16(tokens // cuts, width)] * cuts
    mine, *others = call(scatter_kernel, outs, args, "scatter_rows", "svvvvv" + "v" * (1 + cuts))
    args = [mine] + [shift(other, "core", 1) for other in others]
    grad_out = call(join_kernel, bf16(tokens, width), args, "join_rows", "v" * (cuts + 2))
    grad = exchange(grad_out, CLIP)
    time_saved = forward(hidden, attend_time)
    time_mixed, space_mixed = time_saved[2], hidden[:, width:]
    time_mixed_got, space_mixed_got = shift(time_mixed, "core", 1), shift(space_mixed, "core", 1)
    grad_hidden = backward(
        grad, hidden, time_saved[0], time_saved[1], attend_time, output_time, "time_backward", 60
    )
    half = bf16(tokens, width // 2)
    time_mine, time_other, space_mine, space_other = call(
        lambda *refs: split_kernel(chips, *refs),
        [half] * 4,
        [place, grad, grad_hidden],
        "split_features",
        "svvvvvv",
    )
    args = [time_mine, time_mixed, shift(time_other, "core", 1), time_mixed_got]
    args += [space_mine, space_mixed, shift(space_other, "core", 1), space_mixed_got]
    packed = pack(args, lax.axis_size(("z", "space")))
    grad_hidden = exchange(grad_hidden, CLIP)
    packed = after(packed, grad_hidden)
    packed = lax.all_to_all(packed, ("z", "space"), split_axis=0, concat_axis=0, tiled=True)
    share = jax.ShapeDtypeStruct((SHARE, WIDE), jnp.float32)
    space_grad, time_grad = call(unpack_kernel, [share, share], [packed], "sum_shares", "vvv")
    token_grad = backward(
        grad_hidden, stream, space_saved[0], space_saved[1], attend_space, output_space, "space_backward", 40
    )
    return (token_grad[None], space_grad, time_grad)


def solution(mesh):
    chips = mesh.shape["tm"] // 2
    fine = Mesh(mesh.devices.reshape(chips, 2, mesh.shape["space"]), ("z", "core", "space"))
    whole = ("z", "core", "space")
    in_specs = (
        P(whole, None, None),
        P(OWNERS, "space", None, None, None),
        P(OWNERS, "space", None, None),
        P(OWNERS, "space", None),
        P(),
        P(),
        P(),
        P(),
    )
    out_specs = (P(whole, None, None), P(whole, None), P(whole, None))
    return jax.shard_map(body, mesh=fine, in_specs=in_specs, out_specs=out_specs, check_vma=False)
```

```python
import jax
import jax.numpy as jnp
from jax import lax
from jax.experimental import pallas as pl
from jax.experimental.pallas import tpu as pltpu
from jax.sharding import Mesh
from jax.sharding import PartitionSpec as P

HEADS = 8
HEAD = 88
WIDE = HEADS * HEAD
EPS = 1e-05
PATCHES = 8
SHARE = 11
CUT = 640
CLIP = ("core", "space")
OWNERS = ("z", "core")
ATTEND_CUTS = ((0, 768), (768, 1344))
VMEM = pl.BlockSpec(memory_space=pltpu.VMEM)
SMEM = pl.BlockSpec(memory_space=pltpu.SMEM)
ANY = pl.BlockSpec(memory_space=pl.ANY)


def bf16(*shape):
    return jax.ShapeDtypeStruct(shape, jnp.bfloat16)


def held(*shape):
    return pltpu.VMEM(shape, jnp.bfloat16)


def call(kernel, outs, args, name, spaces, scratch=(), flops=1e6, room=20):
    spec = {"s": SMEM, "v": VMEM, "a": ANY}
    spaces = [spec[c] for c in spaces]
    many = isinstance(outs, list)
    return pl.pallas_call(
        kernel,
        out_shape=outs,
        in_specs=spaces[: len(args)],
        out_specs=spaces[len(args) :] if many else spaces[-1],
        scratch_shapes=scratch,
        compiler_params=pltpu.CompilerParams(vmem_limit_bytes=room * 2**20),
        cost_estimate=pl.CostEstimate(
            flops=int(flops), bytes_accessed=int(flops / 200), transcendentals=0
        ),
        name=name,
    )(*args)


def normalise(stream):
    widened = stream.astype(jnp.float32)
    center = jnp.mean(widened, axis=-1, keepdims=True)
    centered = widened - center
    variance = jnp.mean(centered * centered, axis=-1, keepdims=True)
    scale = lax.rsqrt(variance + EPS)
    return centered * scale, scale


def dot_nt(a, b):
    return lax.dot_general(a, b, (((1,), (1,)), ((), ())), preferred_element_type=jnp.float32)


def dot_tn(a, b):
    return lax.dot_general(a, b, (((0,), (0,)), ((), ())), preferred_element_type=jnp.float32)


def dot_nn(a, b):
    return jnp.dot(a, b, preferred_element_type=jnp.float32)


def same_patch(tokens):
    row = lax.broadcasted_iota(jnp.int32, (tokens, tokens), 0)
    column = lax.broadcasted_iota(jnp.int32, (tokens, tokens), 1)
    return (row % PATCHES) == (column % PATCHES)


def head(projected_ref, part, h):
    at = (part * HEADS + h) * HEAD
    return projected_ref[:, at : at + HEAD]


def forward_kernel(temporal, *refs):
    if temporal:
        stream_in, attend_in, saved_out, mixed_out = refs[:4]
        stream, attend, saved, mixed, sems = refs[4:]
    else:
        stream_in, attend_in, output_in, saved_out, result_out = refs[:5]
        stream, attend, saved, output, result, sems = refs[5:]
        mixed = result.at[:, pl.ds(stream.shape[1], WIDE)]
    width, tokens = stream.shape[1], stream.shape[0]
    projected = saved.at[:, pl.ds(HEADS * tokens, 3 * WIDE)]

    def copy(source, target, at):
        return pltpu.make_async_copy(source, target, sems.at[at])

    load = copy(stream_in.at[:, pl.ds(0, width)] if temporal else stream_in, stream, 0)
    load.start()
    parts = [
        copy(attend_in.at[pl.ds(a, n)], attend.at[pl.ds(a, n)], 1 + i)
        for i, (a, n) in enumerate(ATTEND_CUTS)
    ]
    for part in parts:
        part.start()
    if not temporal:
        load_output = copy(output_in, output, 4)
        load_output.start()
    load.wait()
    normed = normalise(stream[...])[0].astype(jnp.bfloat16)
    for part, (a, n) in zip(parts, ATTEND_CUTS):
        part.wait()
        projected[:, a : a + n] = dot_nt(normed, attend[a : a + n, :]).astype(jnp.bfloat16)
    if temporal:
        allowed = same_patch(tokens)
    ahead = dot_nt(head(projected, 0, 0), head(projected, 1, 0))
    for h in range(HEADS):
        scores = ahead * HEAD**-0.5
        if h + 1 < HEADS:
            ahead = dot_nt(head(projected, 0, h + 1), head(projected, 1, h + 1))
        if temporal:
            scores = jnp.where(allowed, scores, -jnp.inf)
        weights = jnp.exp(scores - jnp.max(scores, axis=-1, keepdims=True))
        chances = (weights / jnp.sum(weights, axis=-1, keepdims=True)).astype(jnp.bfloat16)
        saved[:, h * tokens : (h + 1) * tokens] = chances
        mixed[:, h * HEAD : (h + 1) * HEAD] = dot_nn(chances, head(projected, 2, h)).astype(
            jnp.bfloat16
        )
    stores = [copy(saved, saved_out, 5)]
    stores[0].start()
    if temporal:
        stores.append(copy(mixed, mixed_out, 6))
    else:
        load_output.wait()
        branch = dot_nn(mixed[...], output[...])
        result[:, :width] = (stream[...].astype(jnp.float32) + branch).astype(jnp.bfloat16)
        stores.append(copy(result, result_out, 6))
    stores[1].start()
    for store in stores:
        store.wait()


def forward(stream, attend, output=None):
    temporal = output is None
    tokens, width = stream.shape[0], attend.shape[0]
    last = (tokens, WIDE) if temporal else (tokens, width + WIDE)
    shapes = [(tokens, HEADS * tokens + 3 * WIDE), last]
    outs = [bf16(*shape) for shape in shapes]
    scratch = [held(tokens, width), held(3 * WIDE, width)] + [held(*shape) for shape in shapes]
    args = [stream, attend.T]
    if not temporal:
        args.append(output.T)
        scratch.insert(3, held(WIDE, width))
    scratch.append(pltpu.SemaphoreType.DMA((16,)))
    name = "time_forward" if temporal else "space_forward"
    spaces = "a" * (len(args) + len(outs))
    return call(lambda *refs: forward_kernel(temporal, *refs), outs, args, name, spaces, scratch, 2.2e9, 60)


def backward_kernel(
    grad_in, stream_in, saved_in, attend_in, output_in, result_out,
    grad, stream, saved, attend, output, result, dproj, sems,
):
    bf = jnp.bfloat16

    def copy(source, target, at):
        return pltpu.make_async_copy(source, target, sems.at[at])

    load_grad, load_output = copy(grad_in, grad, 0), copy(output_in, output, 1)
    load_saved = copy(saved_in, saved, 2)
    tokens = grad.shape[0]
    projected = saved.at[:, pl.ds(HEADS * tokens, 3 * WIDE)]
    load_attend, load_stream = copy(attend_in, attend, 3), copy(stream_in.at[:, pl.ds(0, stream.shape[1])], stream, 4)
    for load in (load_grad, load_output, load_saved, load_attend, load_stream):
        load.start()
    load_grad.wait()
    load_output.wait()
    dmixed = dot_nt(grad[...], output[...]).astype(bf)
    load_saved.wait()
    for h in range(HEADS):
        chances = saved[:, h * tokens : (h + 1) * tokens]
        dm = dmixed[:, h * HEAD : (h + 1) * HEAD]
        dprobs = dot_nt(dm, head(projected, 2, h)).astype(bf).astype(jnp.float32)
        wide = chances.astype(jnp.float32)
        scaled = wide * dprobs
        dscores = (scaled - wide * jnp.sum(scaled, axis=-1, keepdims=True)) * HEAD**-0.5
        dscores = dscores.astype(bf)
        for part, value in (
            (0, dot_nn(dscores, head(projected, 1, h))),
            (1, dot_tn(dscores, head(projected, 0, h))),
            (2, dot_tn(chances, dm)),
        ):
            at = (part * HEADS + h) * HEAD
            dproj[:, at : at + HEAD] = value.astype(bf)
    load_attend.wait()
    load_stream.wait()
    tokens = grad.shape[0]
    for i in range(2):
        rows = slice(i * tokens // 2, (i + 1) * tokens // 2)
        dnormed = dot_nn(dproj[rows, :], attend[...]).astype(bf).astype(jnp.float32)
        normed, scale = normalise(stream[rows, :])
        mean_d = jnp.mean(dnormed, axis=-1, keepdims=True)
        mean_dn = jnp.mean(dnormed * normed, axis=-1, keepdims=True)
        inner = scale * (dnormed - mean_d - normed * mean_dn)
        result[rows, :] = (grad[rows, :].astype(jnp.float32) + inner).astype(bf)
    store = copy(result, result_out, 5)
    store.start()
    store.wait()


def backward(grad, stream, saved, attend, output, name, room):
    args = [grad, stream, saved, attend.T, output.T]
    scratch = [held(*arg.shape) for arg in [grad, grad] + args[2:] + [grad]]
    scratch.append(held(grad.shape[0], 3 * WIDE))
    scratch.append(pltpu.SemaphoreType.DMA((16,)))
    return call(backward_kernel, bf16(*grad.shape), args, name, "a" * 6, scratch, 2.6e9, room)


def aim_kernel(counts_ref, targets_in, rows_in, keep_ref, next_ref, last_ref, targets, sems):
    chips = rows_in.shape[0]
    own = lax.axis_index("z")
    far = (own + 2) % chips
    near = ((keep_ref, own), (next_ref, (own + 1) % chips), (last_ref, (own + chips - 1) % chips))
    loads = [pltpu.make_async_copy(targets_in, targets, sems.at[0])]
    for i, (ref, to) in enumerate(near):
        loads.append(pltpu.make_async_copy(rows_in.at[to], ref.at[pl.ds(0, 128)], sems.at[1 + i]))
    for i, ref in enumerate((next_ref, last_ref)):
        source = rows_in.at[far, pl.ds(64 * i, 64)]
        loads.append(pltpu.make_async_copy(source, ref.at[pl.ds(144, 64)], sems.at[4 + i]))
    for load in loads:
        load.start()
    line = lax.broadcasted_iota(jnp.int32, (16, 64), 0)
    slot = lax.broadcasted_iota(jnp.int32, (16, 64), 1)
    loads[0].wait()
    for ref, to, at in [(ref, to, 128) for ref, to in near] + [(next_ref, far, 208), (last_ref, far, 208)]:
        aims = jnp.full((16, 64), -1, jnp.int32)
        for core in range(2):
            valid = (line == core) & (slot < counts_ref[0, 0, 2 * to + core])
            aims = jnp.where(valid, targets[0, 0, pl.ds(2 * to + core, 1), :], aims)
        ref[at : at + 16, :] = jnp.zeros((16, ref.shape[1]), jnp.bfloat16)
        ref[at : at + 16, :64] = aims.astype(jnp.float32).astype(jnp.bfloat16)
    for load in loads[1:]:
        load.wait()


def scatter_kernel(place_ref, keep_ref, next_ref, last_ref, far0_ref, far1_ref, mine_ref, *other_refs):
    tokens = mine_ref.shape[0]
    line = lax.broadcasted_iota(jnp.int32, (16, 64), 0)
    token = lax.broadcasted_iota(jnp.int32, (tokens, 64), 0).astype(jnp.float32)
    for out_refs, core in ((other_refs, 1 - place_ref[1]), ((mine_ref,), place_ref[1])):
        at = pl.multiple_of(core * 64, 64)
        terms = [(ref[128:144, :64], ref[pl.ds(at, 64), :]) for ref in (keep_ref, next_ref, last_ref)]
        terms.append(
            (
                jnp.where(core == 0, far0_ref[64:80, :64], far1_ref[64:80, :64]),
                jnp.where(core == 0, far0_ref[:64, :], far1_ref[:64, :]),
            )
        )
        total = jnp.zeros(mine_ref.shape, jnp.float32)
        for info, rows in terms:
            info = info.astype(jnp.float32)
            aims = jnp.sum(jnp.where(line == core, info, 0.0), axis=0, keepdims=True)
            matches = jnp.where(aims == token, 1.0, 0.0).astype(jnp.bfloat16)
            total = total + dot_nn(matches, rows)
        step = tokens // len(out_refs)
        for i, out_ref in enumerate(out_refs):
            out_ref[...] = total[i * step : (i + 1) * step].astype(jnp.bfloat16)


def join_kernel(mine_ref, *refs):
    got_refs, out_ref = refs[:-1], refs[-1]
    step = mine_ref.shape[0] // len(got_refs)
    for i, got_ref in enumerate(got_refs):
        rows = slice(i * step, (i + 1) * step)
        out_ref[rows, :] = mine_ref[rows, :] + got_ref[...]


def halves_of(grad, chips):
    step = grad.shape[1] // (2 * chips)
    return [
        jnp.concatenate([grad[:, (2 * z + c) * step : (2 * z + c + 1) * step] for z in range(chips)], axis=1)
        for c in range(2)
    ]


def split_kernel(chips, place_ref, *refs):
    first = place_ref[1] == 0
    for grad_ref, mine_ref, other_ref in (refs[:1] + refs[2:4], refs[1:2] + refs[4:6]):
        halves = halves_of(grad_ref[...], chips)
        mine_ref[...] = jnp.where(first, halves[0], halves[1])
        other_ref[...] = jnp.where(first, halves[1], halves[0])


def pack_kernel(*refs):
    packed_out, packed, sems = refs[8:]
    time, space = (
        dot_tn(grad[...], mixed[...]) + dot_tn(grad_got[...], mixed_got[...])
        for grad, mixed, grad_got, mixed_got in (refs[:4], refs[4:8])
    )
    main = jnp.concatenate([time[:, :CUT], space[:, :384]], axis=1)
    left = jnp.concatenate([space[:, 384:CUT], time[:, CUT:], space[:, CUT:]], axis=1)
    zero = jnp.zeros((2, 128), jnp.float32)
    blocks, stores = packed.shape[0], []
    for k in range(blocks):
        x = left[k * SHARE : (k + 1) * SHARE, :]
        cut = [x[:, 128 * t : 128 * (t + 1)] for t in range(3)]
        low = [part[5 * u : 5 * u + 5] for part in cut for u in range(2)]
        low.append(jnp.concatenate([part[10:] for part in cut] + [zero], axis=0))
        low.append(jnp.zeros((5, 128), jnp.float32))
        rows = [main[k * SHARE : (k + 1) * SHARE, :], jnp.concatenate(low, axis=1)]
        packed[k] = jnp.concatenate(rows, axis=0).astype(jnp.bfloat16)
        if (k + 1) % 16 == 0:
            at = pl.ds(k - 15, 16)
            stores.append(pltpu.make_async_copy(packed.at[at], packed_out.at[at], sems.at[k // 16]))
            stores[-1].start()
    for store in stores:
        store.wait()


def pack(arrays, blocks):
    scratch = [held(blocks, 16, 1024), pltpu.SemaphoreType.DMA((blocks // 16,))]
    return call(pack_kernel, bf16(blocks, 16, 1024), arrays, "pack_shares", "vvvvvvvva", scratch)


def unpack_kernel(parts_ref, space_ref, time_ref):
    total = parts_ref[0].astype(jnp.float32)
    for k in range(1, parts_ref.shape[0]):
        total = total + parts_ref[k].astype(jnp.float32)
    low = [total[SHARE:, 128 * t : 128 * (t + 1)] for t in range(7)]
    left = [
        jnp.concatenate([low[2 * t], low[2 * t + 1], low[6][t : t + 1]], axis=0) for t in range(3)
    ]
    time_ref[...] = jnp.concatenate([total[:SHARE, :CUT], left[2][:, :64]], axis=1)
    space_ref[...] = jnp.concatenate([total[:SHARE, CUT:], left[0], left[1], left[2][:, 64:]], axis=1)


def exchange(tokens, axes):
    devices = lax.axis_size(axes)
    cut = tokens.reshape(devices, tokens.shape[0] // devices, tokens.shape[1])
    return lax.all_to_all(cut, axes, split_axis=0, concat_axis=0, tiled=True).reshape(tokens.shape)


def shift(array, axis, by):
    devices = lax.axis_size(axis)
    return lax.ppermute(array, axis, [(i, (i + by) % devices) for i in range(devices)])


def after(array, *others):
    return lax.optimization_barrier((array, *others))[0]


def body(
    video_tokens, grad_rows, targets, counts, attend_space, output_space, attend_time, output_time
):
    chips = lax.axis_size("z")
    stream = video_tokens[0]
    tokens, width = stream.shape
    place = jnp.stack([lax.axis_index("z"), lax.axis_index("core")]).astype(jnp.int32)

    args = [counts, targets, grad_rows.reshape(chips, 128, width)]
    scratch = [pltpu.VMEM(targets.shape, jnp.int32), pltpu.SemaphoreType.DMA((6,))]
    outs = [bf16(144, width), bf16(224, width), bf16(224, width)]
    keep, to_next, to_last = call(aim_kernel, outs, args, "aim_rows", "saavvv", scratch, room=60)
    from_last, from_next = shift(to_next, "z", 1), shift(to_last, "z", chips - 1)
    far = [shift(from_last[144:], "z", 1), shift(from_next[144:], "z", chips - 1)]

    space_saved = forward(stream, attend_space, output_space)
    hidden = exchange(space_saved[1], CLIP)

    place = after(place, space_saved[1])
    args = [place, keep, from_last, from_next, *far]
    cuts = 2
    outs = [bf16(tokens, width)] + [bf16(tokens // cuts, width)] * cuts
    mine, *others = call(scatter_kernel, outs, args, "scatter_rows", "svvvvv" + "v" * (1 + cuts))
    args = [mine] + [shift(other, "core", 1) for other in others]
    grad_out = call(join_kernel, bf16(tokens, width), args, "join_rows", "v" * (cuts + 2))
    grad = exchange(grad_out, CLIP)
    time_saved = forward(hidden, attend_time)
    time_mixed, space_mixed = time_saved[1], hidden[:, width:]
    time_mixed_got, space_mixed_got = shift(time_mixed, "core", 1), shift(space_mixed, "core", 1)
    grad_hidden = backward(
        grad, hidden, time_saved[0], attend_time, output_time, "time_backward", 60
    )
    half = bf16(tokens, width // 2)
    time_mine, time_other, space_mine, space_other = call(
        lambda *refs: split_kernel(chips, *refs),
        [half] * 4,
        [place, grad, grad_hidden],
        "split_features",
        "svvvvvv",
    )
    args = [time_mine, time_mixed, shift(time_other, "core", 1), time_mixed_got]
    args += [space_mine, space_mixed, shift(space_other, "core", 1), space_mixed_got]
    packed = pack(args, lax.axis_size(("z", "space")))
    grad_hidden = exchange(grad_hidden, CLIP)
    packed = after(packed, grad_hidden)
    packed = lax.all_to_all(packed, ("z", "space"), split_axis=0, concat_axis=0, tiled=True)
    share = jax.ShapeDtypeStruct((SHARE, WIDE), jnp.float32)
    space_grad, time_grad = call(unpack_kernel, [share, share], [packed], "sum_shares", "vvv")
    token_grad = backward(
        grad_hidden, stream, space_saved[0], attend_space, output_space, "space_backward", 40
    )
    return (token_grad[None], space_grad, time_grad)


def solution(mesh):
    chips = mesh.shape["tm"] // 2
    fine = Mesh(mesh.devices.reshape(chips, 2, mesh.shape["space"]), ("z", "core", "space"))
    whole = ("z", "core", "space")
    in_specs = (
        P(whole, None, None),
        P(OWNERS, "space", None, None, None),
        P(OWNERS, "space", None, None),
        P(OWNERS, "space", None),
        P(),
        P(),
        P(),
        P(),
    )
    out_specs = (P(whole, None, None), P(whole, None), P(whole, None))
    return jax.shard_map(body, mesh=fine, in_specs=in_specs, out_specs=out_specs, check_vma=False)
```
